32 devices in a mesh: ens: 2 (over y), tm: 4 (over x, core), space: 4 (over z).
Axes of the slice: x: 2, y: 2, z: 4, core: 2. Of those that a mesh axis runs over, the one named last changes fastest.
Arguments:
- eigvecs: bfloat16 [8, 2, 3, 2048, 256], P(('ens', 'tm'), None, None, 'space'), parts along dimension 0, may hold values from -6 to 6
- links: bfloat16 [8, 3, 2, 3, 3, 2048], P(('ens', 'tm'), None, None, None, None, 'space'), parts along dimension 0, may hold values from -2.5 to 2.5
- momenta: int32 [3, 3], replicated, may hold values from -2 to 2
- perambulators: bfloat16 [8, 2, 256, 256], P(('ens', 'tm')), parts along dimension 0, may hold values from -0.25 to 0.25
Outputs:
- elementals: bfloat16 [8, 256, 3, 2, 256], P(('ens', 'tm'), 'space'), parts along dimension 0
- projected: bfloat16 [8, 4, 256, 3, 2, 256], P(('ens', 'tm'), None, 'space'), parts along dimension 0
The draws below stay inside these ranges and needn't reach their ends.
There are 2 independent parts, one for each index of `ens`. The reference program is written for one: setup_inputs(seed, part) draws one part's arguments, and reference() takes and returns one part's arrays. A program takes and returns all parts, laid end to end along the dimension named above; an argument that names none is the same for every part. Nothing has to cross between parts.
All inputs are finite; a program needn't handle non-finite values.
Results may differ from the reference program's by a relative error of at most 0.025.
Values may be sent and summed in bfloat16 or wider, within the bound.
A program may use at most 64 MiB of HBM per device.

```python
import math
import jax
import jax.numpy as jnp
from jax import lax

NEV = 256
LX = 32
LY = 16
SITES = 512
NS = 2048
LZ = 4
TIMES = 4
N_SPACE = 4


def with_ends(drawn, own_key, least, largest):
    place = [jax.random.randint(jax.random.fold_in(own_key, axis), (), 0, length) for axis, length in enumerate(drawn.shape)]
    longest = drawn.shape.index(max(drawn.shape))
    beside = place[:longest] + [(place[longest] + 1) % drawn.shape[longest]] + place[longest + 1:]
    return drawn.at[tuple(place)].set(least).at[tuple(beside)].set(largest)


def shard_levels(rng, extent, pieces, least, top_value):
    def one(dim, blocks):
        heights = jax.random.uniform(jax.random.fold_in(jax.random.fold_in(rng, 6), dim), (blocks,), jnp.float32, least / len(pieces), top_value / len(pieces))
        return jnp.repeat(jnp.exp(heights), extent[dim] // blocks).reshape((-1,) + (1,) * (len(extent) - dim - 1))

    loudness = one(*pieces[0])
    for cut in pieces[1:]:
        loudness = loudness * one(*cut)
    return loudness


def scatter_about(own_key, extent, spread, reach, cuts=(), held_as=jnp.bfloat16):
    level = shard_levels(own_key, extent, cuts, -0.22, 0.18) if cuts else 1.0
    array = jax.random.normal(own_key, extent, jnp.float32) * spread * level
    return jnp.minimum(jnp.maximum(array, -reach), reach).astype(held_as)


def setup_inputs(seed: int = 0, part: int = 0) -> dict:
    seeds = jax.random.split(jax.random.key(seed), 5)
    part_keys = jax.random.split(jax.random.fold_in(seeds[4], part), 5)
    eigvecs = scatter_about(part_keys[0], (TIMES, 2, 3, NS, NEV), 1.0, 6.0, ((0, 4), (3, 4)))
    links = scatter_about(part_keys[1], (TIMES, 3, 2, 3, 3, NS), 0.4, 2.5, ((0, 4), (5, 4)))
    momenta = with_ends(jax.random.randint(seeds[2], (3, 3), -2, 3), jax.random.fold_in(seeds[2], 1), -2, 2).astype(jnp.int32)
    perambulators = scatter_about(part_keys[3], (TIMES, 2, NEV, NEV), (2 * NEV) ** -0.5, 0.25, ((0, 4),))
    return {"eigvecs": eigvecs, "links": links, "momenta": momenta, "perambulators": perambulators}


def color_apply(link_pair, shifted):
    link_real = link_pair[0].astype(jnp.float32)
    link_imag = link_pair[1].astype(jnp.float32)
    moved_real = shifted[0].astype(jnp.float32)
    moved_imag = shifted[1].astype(jnp.float32)
    real_part = jnp.einsum('abs,bsm->asm', link_real, moved_real) - jnp.einsum('abs,bsm->asm', link_imag, moved_imag)
    imag_part = jnp.einsum('abs,bsm->asm', link_real, moved_imag) + jnp.einsum('abs,bsm->asm', link_imag, moved_real)
    return (real_part, imag_part)

def phase_angle(momentum, first_pos, second_pos, third_pos, depth):
    weights = momentum.astype(jnp.float32)
    return 2.0 * math.pi * (weights[0] * first_pos / LX + weights[1] * second_pos / LY + weights[2] * third_pos / depth)

def phased(real_part, imag_part, angle):
    cosine = jnp.cos(angle)[None, :, None]
    sine_value = jnp.sin(angle)[None, :, None]
    phased_real = (cosine * real_part + sine_value * imag_part).astype(jnp.bfloat16)
    phased_imag = (cosine * imag_part - sine_value * real_part).astype(jnp.bfloat16)
    upper = jnp.stack([phased_real, phased_imag], 2)
    lower = jnp.stack([phased_imag, -phased_real], 2)
    return jnp.stack([upper, lower], 0)

def section_elementals(vectors, link_set, momenta):
    lattice = vectors.reshape(2, 3, LZ, LY, LX, NEV)
    shifted = [jnp.roll(lattice, -1, 4), jnp.roll(lattice, -1, 3), jnp.roll(lattice, -1, 2)]
    site_index = jnp.arange(NS, dtype=jnp.int32)
    first_pos = (site_index % LX).astype(jnp.float32)
    second_pos = (site_index // LX % LY).astype(jnp.float32)
    third_pos = (site_index // (LX * LY)).astype(jnp.float32)
    blocks = []
    for momentum_index in range(3):
        real_part, imag_part = color_apply(link_set[momentum_index], shifted[momentum_index].reshape(2, 3, NS, NEV))
        angle = phase_angle(momenta[momentum_index], first_pos, second_pos, third_pos, LZ)
        blocks.append(phased(real_part, imag_part, angle))
    right_side = jnp.stack(blocks, 3)
    norm_factor = 1.0 / math.sqrt(6.0 * NS)

    def add_tile(running, tile_index):
        offset = tile_index * SITES
        left_block = lax.dynamic_slice_in_dim(vectors, offset, SITES, 2).reshape(6 * SITES, NEV)
        right_block = lax.dynamic_slice_in_dim(right_side, offset, SITES, 2).reshape(6 * SITES, 6 * NEV)
        partial_value = lax.dot_general(left_block, right_block, (((0,), (0,)), ((), ())), preferred_element_type=jnp.float32) * norm_factor
        rounded = lax.optimization_barrier(partial_value.astype(jnp.bfloat16))
        return (running + rounded.astype(jnp.float32), None)
    initial = jnp.zeros((NEV, 6 * NEV), jnp.float32)
    summed, _ = lax.scan(add_tile, initial, jnp.arange(N_SPACE, dtype=jnp.int32))
    return summed.astype(jnp.bfloat16).reshape(NEV, 3, 2, NEV)

def right_factor(resident):
    upper = jnp.concatenate([resident[0], resident[1]], 1)
    lower = jnp.concatenate([-resident[1], resident[0]], 1)
    return jnp.concatenate([upper, lower], 0)

def reference(eigvecs, links, momenta, perambulators):

    def one_slice(inputs_pair):
        return section_elementals(inputs_pair[0], inputs_pair[1], momenta)
    elementals = lax.map(one_slice, (eigvecs, links))

    def per_sink(resident):
        factor = right_factor(resident)

        def per_source(elemental):
            flattened = elemental.reshape(NEV * 3, 2 * NEV)
            product = jnp.dot(flattened, factor, preferred_element_type=jnp.float32)
            return product.astype(jnp.bfloat16).reshape(NEV, 3, 2, NEV)
        return lax.map(per_source, elementals)
    projected = lax.map(per_sink, perambulators)
    return (elementals, projected)
```

```python
import functools
import math

import jax
import jax.numpy as jnp
from jax import lax
from jax.experimental import pallas as pl
from jax.experimental.pallas import tpu as pltpu
from jax.sharding import PartitionSpec as P

LX = 32
LY = 16
BATCH = 128
MESH = pl.DeviceIdType.MESH
F32 = jnp.float32
BF16 = jnp.bfloat16


def kernel(n, count, sites, modes, early, mom, links, peram, eig, out_e, out_p, vec, halo, left_t, right, coef,
           columns, acc, part, slots, gathered, local_sem, halo_send, halo_recv, rs_send, rs_recv, ag_send, ag_recv):
    me = lax.axis_index("space")
    my_t = lax.axis_index("tm")
    owned = modes // n
    batches = sites // BATCH
    behind = lax.rem(me + n - 1, n)
    ahead = lax.rem(me + 1, n)
    peers = [lax.rem(my_t + step, count) for step in range(1, count)]

    barrier = pltpu.get_barrier_semaphore()
    for neighbour in (behind, ahead):
        pl.semaphore_signal(barrier, inc=1, device_id={"space": neighbour}, device_id_type=MESH)
    for peer in peers:
        pl.semaphore_signal(barrier, inc=1, device_id={"tm": peer}, device_id_type=MESH)
    locals_ = []
    for c in range(batches):
        rows = pl.ds(c * BATCH, BATCH)
        locals_.append(pltpu.make_async_copy(eig.at[0, :, :, rows], vec.at[:, :, rows], local_sem.at[c]))
    for copy in locals_:
        copy.start()
    pl.semaphore_wait(barrier, 1 + count)

    halos = []
    for c in range(batches):
        rows = pl.ds(c * BATCH, BATCH)
        halos.append(
            pltpu.make_async_remote_copy(
                src_ref=eig.at[0, :, :, rows],
                dst_ref=halo.at[:, :, rows],
                send_sem=halo_send.at[c],
                recv_sem=halo_recv.at[c],
                device_id={"space": behind},
                device_id_type=MESH,
            )
        )
    for copy in halos:
        copy.start()

    site = lax.broadcasted_iota(jnp.int32, (1, sites), 1)
    x_pos = lax.rem(site, LX).astype(F32)
    y_pos = lax.rem(site // LX, LY).astype(F32)
    z_pos = jnp.full((1, sites), me, jnp.int32).astype(F32)
    coef[...] = jnp.zeros_like(coef)
    for k in range(3):
        weights = [mom[k, axis].astype(F32) for axis in range(3)]
        angle = 2.0 * math.pi * (weights[0] * x_pos / LX + weights[1] * y_pos / LY + weights[2] * z_pos / n)
        cosine = jnp.cos(angle)
        sine = jnp.sin(angle)
        for a in range(3):
            link_real = links[0, k, 0, a].astype(F32)
            link_imag = links[0, k, 1, a].astype(F32)
            row = (k * 6 + a) * 4
            coef[row:row + 3, :] = cosine * link_real + sine * link_imag
            row = (k * 6 + 3 + a) * 4
            coef[row:row + 3, :] = cosine * link_imag - sine * link_real
    for c in range(batches):
        rows = pl.ds(c * BATCH, BATCH)
        columns[rows, :] = jnp.transpose(coef[:, rows])

    for copy in locals_:
        copy.wait()
    for r in range(2):
        for a in range(3):
            for c in range(batches):
                rows = pl.ds(c * BATCH, BATCH)
                left_t[r, c, :, a * BATCH:(a + 1) * BATCH] = jnp.transpose(vec[r, a, rows, :].astype(F32)).astype(BF16)

    def displace(k, c):
        def one_row(g, carry):
            strip = c * (BATCH // LX) + g
            source_strip = lax.rem(strip + 1, LY) if k == 1 else strip
            source = halo if k == 2 else vec
            rows = pl.ds(pl.multiple_of(source_strip * LX, LX), LX)
            moved = [[source[r, b, rows, :].astype(F32) for b in range(3)] for r in range(2)]
            if k == 0:
                moved = [[pltpu.roll(m, LX - 1, 0) for m in pair] for pair in moved]
            factors = columns[pl.ds(pl.multiple_of(strip * LX, LX), LX), :]
            for a in range(3):
                real = None
                imag = None
                for b in range(3):
                    place = (k * 6 + a) * 4 + b
                    f_real = factors[:, place:place + 1]
                    f_imag = factors[:, place + 12:place + 13]
                    t_real = f_real * moved[0][b] - f_imag * moved[1][b]
                    t_imag = f_real * moved[1][b] + f_imag * moved[0][b]
                    real = t_real if real is None else real + t_real
                    imag = t_imag if imag is None else imag + t_imag
                to = pl.ds(pl.multiple_of(a * BATCH + g * LX, LX), LX)
                right[0, to, :] = real.astype(BF16)
                right[1, to, :] = imag.astype(BF16)
            return carry

        lax.fori_loop(0, BATCH // LX, one_row, 0)

    def contract(c):
        l_real = left_t[0, c]
        l_imag = left_t[1, c]
        r_real = right[0]
        r_imag = right[1]
        dot = functools.partial(jnp.dot, preferred_element_type=F32)
        acc[0] += dot(l_real, r_real) + dot(l_imag, r_imag)
        acc[1] += dot(l_real, r_imag) - dot(l_imag, r_real)

    norm_factor = 1.0 / math.sqrt(6.0 * sites * n)

    def keep(k):
        for d in range(n):
            for r in range(2):
                part[k, d, r * owned:(r + 1) * owned, :] = acc[r, d * owned:(d + 1) * owned, :] * norm_factor

    def batch(k, c):
        displace(k, c)
        contract(c)

    def clear():
        acc[...] = jnp.zeros_like(acc)

    def hop(k, d, to_slot, to):
        return pltpu.make_async_remote_copy(
            src_ref=slots.at[k, d],
            dst_ref=slots.at[k, to_slot],
            send_sem=rs_send.at[k, d],
            recv_sem=rs_recv.at[k, to_slot],
            device_id={"space": to},
            device_id_type=MESH,
        )

    def add_and_send(k, d, first, to_slot, to):
        @pl.when(first)
        def _():
            slots[k, d] = part[k, d].astype(BF16)

        @pl.when(jnp.logical_not(first))
        def _():
            hop(k, d, d, ahead).wait_recv()
            slots[k, d] = (slots[k, d].astype(F32) + part[k, d]).astype(BF16)

        hop(k, d, to_slot, to).start()

    def pass_on(ks):
        def step(i, carry):
            for k in ks:
                far = n - 1 - i

                @pl.when(far > me)
                def _():
                    add_and_send(k, far, me == 0, far, ahead)

                @pl.when(i < me)
                def _():
                    add_and_send(k, i, me == n - 1, jnp.where(i == me - 1, n, i), behind)

            return carry

        lax.fori_loop(0, n - 1, step, 0)

    def spread(k, peer):
        return pltpu.make_async_remote_copy(
            src_ref=gathered.at[my_t, k],
            dst_ref=gathered.at[my_t, k],
            send_sem=ag_send.at[k, peer],
            recv_sem=ag_recv.at[k, my_t],
            device_id={"tm": peer},
            device_id_type=MESH,
        )

    def finish(k):
        @pl.when(me > 0)
        def _():
            hop(k, me, me, ahead).wait_recv()
            part[k, me] += slots[k, me].astype(F32)

        @pl.when(me < n - 1)
        def _():
            hop(k, n, n, ahead).wait_recv()
            part[k, me] += slots[k, n].astype(F32)

        gathered[my_t, k] = part[k, me].astype(BF16)
        for peer in peers:
            spread(k, peer).start()

    def project_one(k, t):
        rows = gathered[t, k]
        with_real = jnp.dot(rows, peram[0, 0], preferred_element_type=F32)
        with_imag = jnp.dot(rows, peram[0, 1], preferred_element_type=F32)
        lane = k * 2 * modes
        out_p[t, :, lane:lane + modes] = (with_real[:owned] - with_imag[owned:]).astype(BF16)
        out_p[t, :, lane + modes:lane + 2 * modes] = (with_imag[:owned] + with_real[owned:]).astype(BF16)

    def project(k):
        for r in range(2):
            lane = (k * 2 + r) * modes
            out_e[:, lane:lane + modes] = gathered[my_t, k, r * owned:(r + 1) * owned, :]
        project_one(k, my_t)
        for peer in peers:
            pltpu.make_async_remote_copy(
                src_ref=gathered.at[peer, k],
                dst_ref=gathered.at[peer, k],
                send_sem=ag_send.at[k, peer],
                recv_sem=ag_recv.at[k, peer],
                device_id={"tm": peer},
                device_id_type=MESH,
            ).wait_recv()
            project_one(k, peer)

    for k in range(2):
        clear()
        for c in range(batches):
            batch(k, c)
        keep(k)
    clear()
    for c in range(batches):
        if c == early:
            pass_on((0, 1))
            finish(0)
            finish(1)
        halos[c].wait_recv()
        batch(2, c)
    keep(2)
    if early >= batches:
        pass_on((0, 1))
    pass_on((2,))
    if early >= batches:
        finish(0)
        finish(1)
    project(0)
    project(1)
    finish(2)
    project(2)

    for copy in halos:
        copy.wait_send()
    for k in range(3):
        def sent(d, carry, k=k):
            @pl.when(d != me)
            def _():
                hop(k, d, d, ahead).wait_send()

            return carry

        lax.fori_loop(0, n, sent, 0)
        for peer in peers:
            spread(k, peer).wait_send()


def body(eigvecs, links, momenta, perambulators):
    n = lax.axis_size("space")
    count = lax.axis_size("tm")
    sites, modes = eigvecs.shape[3:]
    owned = modes // n
    batches = sites // BATCH
    vmem = pl.BlockSpec(memory_space=pltpu.VMEM)
    elementals, projected = pl.pallas_call(
        functools.partial(kernel, n, count, sites, modes, 2),
        out_shape=(
            jax.ShapeDtypeStruct((owned, 6 * modes), BF16),
            jax.ShapeDtypeStruct((count, owned, 6 * modes), BF16),
        ),
        in_specs=[pl.BlockSpec(memory_space=pltpu.SMEM), vmem, vmem, pl.BlockSpec(memory_space=pl.ANY)],
        out_specs=(vmem, vmem),
        scratch_shapes=[
            pltpu.VMEM((2, 3, sites, modes), BF16),
            pltpu.VMEM((2, 3, sites, modes), BF16),
            pltpu.VMEM((2, batches, modes, 3 * BATCH), BF16),
            pltpu.VMEM((2, 3 * BATCH, modes), BF16),
            pltpu.VMEM((128, sites), F32),
            pltpu.VMEM((sites, 128), F32),
            pltpu.VMEM((2, modes, modes), F32),
            pltpu.VMEM((3, n, 2 * owned, modes), F32),
            pltpu.VMEM((3, n + 1, 2 * owned, modes), BF16),
            pltpu.VMEM((count, 3, 2 * owned, modes), BF16),
            pltpu.SemaphoreType.DMA((batches,)),
            pltpu.SemaphoreType.DMA((batches,)),
            pltpu.SemaphoreType.DMA((batches,)),
            pltpu.SemaphoreType.DMA((3, n + 1)),
            pltpu.SemaphoreType.DMA((3, n + 1)),
            pltpu.SemaphoreType.DMA((3, count)),
            pltpu.SemaphoreType.DMA((3, count)),
        ],
        compiler_params=pltpu.CompilerParams(
            collective_id=0, has_side_effects=True, vmem_limit_bytes=40 * 1024 * 1024
        ),
    )(momenta, links, perambulators, eigvecs)
    return (
        elementals.reshape(1, owned, 3, 2, modes),
        projected.reshape(1, count, owned, 3, 2, modes),
    )


def solution(mesh):
    in_specs = (
        P(("ens", "tm"), None, None, "space", None),
        P(("ens", "tm"), None, None, None, None, "space"),
        P(),
        P(("ens", "tm"), None, None, None),
    )
    out_specs = (
        P(("ens", "tm"), "space", None, None, None),
        P(("ens", "tm"), None, "space", None, None, None),
    )
    return jax.shard_map(body, mesh=mesh, in_specs=in_specs, out_specs=out_specs, check_vma=False)
```

```python
import functools
import math

import jax
import jax.numpy as jnp
from jax import lax
from jax.experimental import pallas as pl
from jax.experimental.pallas import tpu as pltpu
from jax.sharding import PartitionSpec as P

LX = 32
LY = 16
BATCH = 128
MESH = pl.DeviceIdType.MESH
F32 = jnp.float32
BF16 = jnp.bfloat16


def kernel(n, count, sites, modes, mom_in, links_in, peram_in, eig, out_e, out_p, mom, links, peram, vec, halo, left_t,
           right, coef, columns, acc, part, slots, outgoing, direct, gathered, held, in_sem, vec_sem, halo_send, halo_recv,
           rs_send, rs_recv, last_send, last_recv, ag_send, ag_recv):
    me = lax.axis_index("space")
    my_t = lax.axis_index("tm")
    owned = modes // n
    half = modes // 2
    batches = sites // BATCH
    behind = lax.rem(me + n - 1, n)
    ahead = lax.rem(me + 1, n)
    others = [lax.rem(me + step, n) for step in range(1, n)]
    peers = [lax.rem(my_t + step, count) for step in range(1, count)]
    groups = ((0, 4), (4, 1), (5, 1))

    barrier = pltpu.get_barrier_semaphore()
    for other in others:
        pl.semaphore_signal(barrier, inc=1, device_id={"space": other}, device_id_type=MESH)
    for peer in peers:
        pl.semaphore_signal(barrier, inc=1, device_id={"tm": peer}, device_id_type=MESH)
    load_mom = pltpu.make_async_copy(mom_in, mom, in_sem.at[0])
    load_links = pltpu.make_async_copy(links_in, links, in_sem.at[1])
    load_peram = pltpu.make_async_copy(peram_in, peram, in_sem.at[2])
    load_vec = pltpu.make_async_copy(eig.at[0], vec, vec_sem)
    for copy in (load_mom, load_links, load_vec, load_peram):
        copy.start()
    pl.semaphore_wait(barrier, n + count - 2)

    halos = [[], []]
    for h in range(2):
        for c in range(batches):
            rows = pl.ds(c * BATCH, BATCH)
            halos[h].append(
                pltpu.make_async_remote_copy(
                    src_ref=eig.at[0, :, :, rows, pl.ds(h * half, half)],
                    dst_ref=halo.at[h, :, :, rows],
                    send_sem=halo_send.at[h, c],
                    recv_sem=halo_recv.at[h, c],
                    device_id={"space": behind},
                    device_id_type=MESH,
                )
            )
    for copy in halos[0] + halos[1]:
        copy.start()

    site = lax.broadcasted_iota(jnp.int32, (1, sites), 1)
    x_pos = lax.rem(site, LX).astype(F32)
    y_pos = lax.rem(site // LX, LY).astype(F32)
    z_pos = jnp.full((1, sites), me, jnp.int32).astype(F32)
    coef[...] = jnp.zeros_like(coef)
    load_mom.wait()
    load_links.wait()
    for k in range(3):
        weights = [mom[k, axis].astype(F32) for axis in range(3)]
        angle = 2.0 * math.pi * (weights[0] * x_pos / LX + weights[1] * y_pos / LY + weights[2] * z_pos / n)
        cosine = jnp.cos(angle)
        sine = jnp.sin(angle)
        for a in range(3):
            for b in range(3):
                pair = links[0, k, a, b].astype(F32)
                row = ((k * 3 + a) * 3 + b) * 2
                coef[row:row + 1, :] = cosine * pair[0:1] + sine * pair[1:2]
                coef[row + 1:row + 2, :] = cosine * pair[1:2] - sine * pair[0:1]
    for c in range(batches):
        rows = pl.ds(c * BATCH, BATCH)
        columns[rows, :] = jnp.transpose(coef[:, rows])

    load_vec.wait()
    for r in range(2):
        for a in range(3):
            for c in range(batches):
                rows = pl.ds(c * BATCH, BATCH)
                left_t[r, c, :, a * BATCH:(a + 1) * BATCH] = jnp.transpose(vec[r, a, rows, :].astype(F32)).astype(BF16)

    def displace(k, c, read, width):
        def one_row(g, carry):
            strip = c * (BATCH // LX) + g
            source_strip = lax.rem(strip + 1, LY) if k == 1 else strip
            rows = pl.ds(pl.multiple_of(source_strip * LX, LX), LX)
            moved = [[read(r, b, rows).astype(F32) for b in range(3)] for r in range(2)]
            if k == 0:
                moved = [[pltpu.roll(m, LX - 1, 0) for m in pair] for pair in moved]
            factors = columns[pl.ds(pl.multiple_of(strip * LX, LX), LX), :]
            for a in range(3):
                real = None
                imag = None
                for b in range(3):
                    place = ((k * 3 + a) * 3 + b) * 2
                    f_real = factors[:, place:place + 1]
                    f_imag = factors[:, place + 1:place + 2]
                    t_real = f_real * moved[0][b] - f_imag * moved[1][b]
                    t_imag = f_real * moved[1][b] + f_imag * moved[0][b]
                    real = t_real if real is None else real + t_real
                    imag = t_imag if imag is None else imag + t_imag
                to = pl.ds(pl.multiple_of(a * BATCH + g * LX, LX), LX)
                right[0, to, :width] = real.astype(BF16)
                right[1, to, :width] = imag.astype(BF16)
            return carry

        lax.fori_loop(0, BATCH // LX, one_row, 0)

    def contract(c, width):
        l_real = left_t[0, c]
        l_imag = left_t[1, c]
        r_real = right[0, :, :width]
        r_imag = right[1, :, :width]
        dot = functools.partial(jnp.dot, preferred_element_type=F32)
        real = dot(l_real, r_real) + dot(l_imag, r_imag)
        imag = dot(l_real, r_imag) - dot(l_imag, r_real)
        if c == 0:
            acc[0, :, :width] = real
            acc[1, :, :width] = imag
        else:
            acc[0, :, :width] += real
            acc[1, :, :width] += imag

    norm_factor = 1.0 / math.sqrt(6.0 * sites * n)

    def keep(piece, lane):
        for d in range(n):
            for r in range(2):
                part[d, piece, r * owned:(r + 1) * owned, :] = (
                    acc[r, d * owned:(d + 1) * owned, lane:lane + half] * norm_factor
                )

    def hop(g, d, to_slot, to):
        pieces = pl.ds(*groups[g])
        return pltpu.make_async_remote_copy(
            src_ref=slots.at[d, pieces],
            dst_ref=slots.at[to_slot, pieces],
            send_sem=rs_send.at[g, d],
            recv_sem=rs_recv.at[g, to_slot],
            device_id={"space": to},
            device_id_type=MESH,
        )

    def add_and_send(g, d, first, to_slot, to):
        pieces = pl.ds(*groups[g])

        @pl.when(first)
        def _():
            slots[d, pieces] = part[d, pieces].astype(BF16)

        @pl.when(jnp.logical_not(first))
        def _():
            hop(g, d, d, ahead).wait_recv()
            slots[d, pieces] = (slots[d, pieces].astype(F32) + part[d, pieces]).astype(BF16)

        hop(g, d, to_slot, to).start()

    def turns(g, low, high):
        def turn(s, carry):
            @pl.when(me <= s)
            def _():
                far = n - 1 - s + me
                add_and_send(g, far, me == 0, far, ahead)

            @pl.when(n - 1 - me <= s)
            def _():
                near = s - (n - 1 - me)
                add_and_send(g, near, me == n - 1, jnp.where(near == me - 1, n, near), behind)

            return carry

        lax.fori_loop(min(low, n - 1), min(high, n - 1), turn, 0)

    def to_all(d):
        return pltpu.make_async_remote_copy(
            src_ref=outgoing.at[d],
            dst_ref=direct.at[me],
            send_sem=last_send.at[d],
            recv_sem=last_recv.at[me],
            device_id={"space": d},
            device_id_type=MESH,
        )

    def spread(g, t, peer):
        pieces = pl.ds(*groups[g])
        return pltpu.make_async_remote_copy(
            src_ref=gathered.at[t, pieces],
            dst_ref=gathered.at[t, pieces],
            send_sem=ag_send.at[g, peer],
            recv_sem=ag_recv.at[g, t],
            device_id={"tm": peer},
            device_id_type=MESH,
        )

    def give_out(g):
        pieces = pl.ds(*groups[g])
        gathered[my_t, pieces] = part[me, pieces].astype(BF16)
        for peer in peers:
            spread(g, my_t, peer).start()

    def finish(g):
        pieces = pl.ds(*groups[g])

        @pl.when(me > 0)
        def _():
            hop(g, me, me, ahead).wait_recv()
            part[me, pieces] += slots[me, pieces].astype(F32)

        @pl.when(me < n - 1)
        def _():
            hop(g, n, n, ahead).wait_recv()
            part[me, pieces] += slots[n, pieces].astype(F32)

        give_out(g)

    def project_one(g, t):
        low, size = groups[g]
        for piece in range(low, low + size, 2):
            k = piece // 2
            with_real = None
            for p in range(piece, min(piece + 2, low + size)):
                at = (p % 2) * half
                rows = gathered[t, p]
                by_real = jnp.dot(rows, peram[0, 0, at:at + half, :], preferred_element_type=F32)
                by_imag = jnp.dot(rows, peram[0, 1, at:at + half, :], preferred_element_type=F32)
                with_real = by_real if with_real is None else with_real + by_real
                with_imag = by_imag if p == piece else with_imag + by_imag
            real = with_real[:owned] - with_imag[owned:]
            imag = with_imag[:owned] + with_real[owned:]
            if g == 1:
                held[t, 0] = real
                held[t, 1] = imag
                continue
            if g == 2:
                real += held[t, 0]
                imag += held[t, 1]
            lane = k * 2 * modes
            out_p[t, :, lane:lane + modes] = real.astype(BF16)
            out_p[t, :, lane + modes:lane + 2 * modes] = imag.astype(BF16)

    def project(g):
        low, size = groups[g]
        for p in range(low, low + size):
            for r in range(2):
                lane = (p // 2 * 2 + r) * modes + (p % 2) * half
                out_e[:, lane:lane + half] = gathered[my_t, p, r * owned:(r + 1) * owned, :]
        project_one(g, my_t)
        for peer in peers:
            spread(g, peer, peer).wait_recv()
            project_one(g, peer)

    def whole_width(r, b, rows):
        return vec[r, b, rows, :]

    def batch(h, c):
        halos[h][c].wait_recv()
        displace(2, c, lambda r, b, rows: halo[h, r, b, rows, :], half)
        contract(c, half)

    for k in range(2):
        for c in range(batches):
            displace(k, c, whole_width, modes)
            contract(c, modes)
        keep(2 * k, 0)
        keep(2 * k + 1, half)
    turns(0, 0, 1)
    for c in range(batches):
        batch(0, c)
        if c == batches // 2 - 1:
            turns(0, 1, 2)
    keep(4, 0)
    turns(0, 2, n - 1)
    turns(1, 0, 1)
    finish(0)
    load_peram.wait()
    for c in range(batches):
        batch(1, c)
        if c == 0:
            turns(1, 1, 2)
            project(0)
        if c == 1:
            turns(1, 2, n - 1)
        if c == batches - 2:
            finish(1)
            project(1)
    keep(5, 0)
    for d in others:
        outgoing[d] = part[d, 5].astype(BF16)
        to_all(d).start()
    for d in others:
        pltpu.make_async_remote_copy(
            src_ref=outgoing.at[d],
            dst_ref=direct.at[d],
            send_sem=last_send.at[d],
            recv_sem=last_recv.at[d],
            device_id={"space": d},
            device_id_type=MESH,
        ).wait_recv()
        part[me, 5] += direct[d].astype(F32)
    give_out(2)
    project(2)

    for copy in halos[0] + halos[1]:
        copy.wait_send()
    for d in others:
        for g in range(2):
            hop(g, d, d, ahead).wait_send()
        to_all(d).wait_send()
    for g in range(3):
        for peer in peers:
            spread(g, my_t, peer).wait_send()


def body(eigvecs, links, momenta, perambulators):
    n = lax.axis_size("space")
    count = lax.axis_size("tm")
    sites, modes = eigvecs.shape[3:]
    owned = modes // n
    half = modes // 2
    batches = sites // BATCH
    vmem = pl.BlockSpec(memory_space=pltpu.VMEM)
    hbm = pl.BlockSpec(memory_space=pltpu.HBM)
    moved_links = jnp.transpose(links, (0, 1, 3, 4, 2, 5))
    elementals, projected = pl.pallas_call(
        functools.partial(kernel, n, count, sites, modes),
        out_shape=(
            jax.ShapeDtypeStruct((owned, 6 * modes), BF16),
            jax.ShapeDtypeStruct((count, owned, 6 * modes), BF16),
        ),
        in_specs=[hbm] * 4,
        out_specs=(vmem, vmem),
        scratch_shapes=[
            pltpu.SMEM(momenta.shape, jnp.int32),
            pltpu.VMEM(moved_links.shape, BF16),
            pltpu.VMEM(perambulators.shape, BF16),
            pltpu.VMEM((2, 3, sites, modes), BF16),
            pltpu.VMEM((2, 2, 3, sites, half), BF16),
            pltpu.VMEM((2, batches, modes, 3 * BATCH), BF16),
            pltpu.VMEM((2, 3 * BATCH, modes), BF16),
            pltpu.VMEM((128, sites), F32),
            pltpu.VMEM((sites, 128), F32),
            pltpu.VMEM((2, modes, modes), F32),
            pltpu.VMEM((n, 6, 2 * owned, half), F32),
            pltpu.VMEM((n + 1, 5, 2 * owned, half), BF16),
            pltpu.VMEM((n, 2 * owned, half), BF16),
            pltpu.VMEM((n, 2 * owned, half), BF16),
            pltpu.VMEM((count, 6, 2 * owned, half), BF16),
            pltpu.VMEM((count, 2, owned, modes), F32),
            pltpu.SemaphoreType.DMA((3,)),
            pltpu.SemaphoreType.DMA,
            pltpu.SemaphoreType.DMA((2, batches)),
            pltpu.SemaphoreType.DMA((2, batches)),
            pltpu.SemaphoreType.DMA((2, n + 1)),
            pltpu.SemaphoreType.DMA((2, n + 1)),
            pltpu.SemaphoreType.DMA((n,)),
            pltpu.SemaphoreType.DMA((n,)),
            pltpu.SemaphoreType.DMA((3, count)),
            pltpu.SemaphoreType.DMA((3, count)),
        ],
        compiler_params=pltpu.CompilerParams(
            collective_id=0, has_side_effects=True, vmem_limit_bytes=62 * 1024 * 1024
        ),
    )(momenta, moved_links, perambulators, eigvecs)
    return (
        elementals.reshape(1, owned, 3, 2, modes),
        projected.reshape(1, count, owned, 3, 2, modes),
    )


def solution(mesh):
    in_specs = (
        P(("ens", "tm"), None, None, "space", None),
        P(("ens", "tm"), None, None, None, None, "space"),
        P(),
        P(("ens", "tm"), None, None, None),
    )
    out_specs = (
        P(("ens", "tm"), "space", None, None, None),
        P(("ens", "tm"), None, "space", None, None, None),
    )
    return jax.shard_map(body, mesh=mesh, in_specs=in_specs, out_specs=out_specs, check_vma=False)
```

```python
import functools
import math

import jax
import jax.numpy as jnp
from jax import lax
from jax.experimental import pallas as pl
from jax.experimental.pallas import tpu as pltpu
from jax.sharding import PartitionSpec as P

LX = 32
LY = 16
BATCH = 128
MESH = pl.DeviceIdType.MESH
F32 = jnp.float32
BF16 = jnp.bfloat16


def kernel(n, count, sites, modes, mom_in, links_in, peram_in, eig, out_e, out_p, mom, links, peram, vec, halo, left_t,
           right, coef, columns, acc, part, slots, outgoing, direct, gathered, held, in_sem, vec_sem, halo_send, halo_recv,
           rs_send, rs_recv, last_send, last_recv, ag_send, ag_recv):
    me = lax.axis_index("space")
    my_t = lax.axis_index("tm")
    owned = modes // n
    half = modes // 2
    batches = sites // BATCH
    behind = lax.rem(me + n - 1, n)
    ahead = lax.rem(me + 1, n)
    others = [lax.rem(me + step, n) for step in range(1, n)]
    peers = [lax.rem(my_t + step, count) for step in range(1, count)]
    groups = ((0, 2), (2, 2), (4, 1), (5, 1))

    barrier = pltpu.get_barrier_semaphore()
    for other in others:
        pl.semaphore_signal(barrier, inc=1, device_id={"space": other}, device_id_type=MESH)
    for peer in peers:
        pl.semaphore_signal(barrier, inc=1, device_id={"tm": peer}, device_id_type=MESH)
    load_mom = pltpu.make_async_copy(mom_in, mom, in_sem.at[0])
    load_links = pltpu.make_async_copy(links_in, links, in_sem.at[1])
    load_peram = pltpu.make_async_copy(peram_in, peram, in_sem.at[2])
    load_vec = pltpu.make_async_copy(eig.at[0], vec, vec_sem)
    for copy in (load_mom, load_links, load_vec, load_peram):
        copy.start()
    pl.semaphore_wait(barrier, n + count - 2)

    halos = [[], []]
    for h in range(2):
        for c in range(batches):
            rows = pl.ds(c * BATCH, BATCH)
            halos[h].append(
                pltpu.make_async_remote_copy(
                    src_ref=eig.at[0, :, :, rows, pl.ds(h * half, half)],
                    dst_ref=halo.at[h, :, :, rows],
                    send_sem=halo_send.at[h, c],
                    recv_sem=halo_recv.at[h, c],
                    device_id={"space": behind},
                    device_id_type=MESH,
                )
            )
    waiting = halos[0] + halos[1]

    def send_batches(number):
        for _ in range(min(number, len(waiting))):
            waiting.pop(0).start()

    send_batches(3)

    site = lax.broadcasted_iota(jnp.int32, (1, sites), 1)
    x_pos = lax.rem(site, LX).astype(F32)
    y_pos = lax.rem(site // LX, LY).astype(F32)
    z_pos = jnp.full((1, sites), me, jnp.int32).astype(F32)
    coef[...] = jnp.zeros_like(coef)
    load_mom.wait()
    load_links.wait()
    for k in range(3):
        weights = [mom[k, axis].astype(F32) for axis in range(3)]
        angle = 2.0 * math.pi * (weights[0] * x_pos / LX + weights[1] * y_pos / LY + weights[2] * z_pos / n)
        cosine = jnp.cos(angle)
        sine = jnp.sin(angle)
        for a in range(3):
            for b in range(3):
                pair = links[0, k, a, b].astype(F32)
                row = ((k * 3 + a) * 3 + b) * 2
                coef[row:row + 1, :] = cosine * pair[0:1] + sine * pair[1:2]
                coef[row + 1:row + 2, :] = cosine * pair[1:2] - sine * pair[0:1]
    for c in range(batches):
        rows = pl.ds(c * BATCH, BATCH)
        columns[rows, :] = jnp.transpose(coef[:, rows])

    load_vec.wait()
    for r in range(2):
        for a in range(3):
            for c in range(batches):
                rows = pl.ds(c * BATCH, BATCH)
                left_t[r, c, :, a * BATCH:(a + 1) * BATCH] = jnp.transpose(vec[r, a, rows, :].astype(F32)).astype(BF16)

    def displace(k, c, read, width):
        def one_row(g, carry):
            strip = c * (BATCH // LX) + g
            source_strip = lax.rem(strip + 1, LY) if k == 1 else strip
            rows = pl.ds(pl.multiple_of(source_strip * LX, LX), LX)
            moved = [[read(r, b, rows).astype(F32) for b in range(3)] for r in range(2)]
            if k == 0:
                moved = [[pltpu.roll(m, LX - 1, 0) for m in pair] for pair in moved]
            factors = columns[pl.ds(pl.multiple_of(strip * LX, LX), LX), :]
            for a in range(3):
                real = None
                imag = None
                for b in range(3):
                    place = ((k * 3 + a) * 3 + b) * 2
                    f_real = factors[:, place:place + 1]
                    f_imag = factors[:, place + 1:place + 2]
                    t_real = f_real * moved[0][b] - f_imag * moved[1][b]
                    t_imag = f_real * moved[1][b] + f_imag * moved[0][b]
                    real = t_real if real is None else real + t_real
                    imag = t_imag if imag is None else imag + t_imag
                to = pl.ds(pl.multiple_of(a * BATCH + g * LX, LX), LX)
                right[0, to, :width] = real.astype(BF16)
                right[1, to, :width] = imag.astype(BF16)
            return carry

        lax.fori_loop(0, BATCH // LX, one_row, 0)

    def contract(c, width):
        l_real = left_t[0, c]
        l_imag = left_t[1, c]
        r_real = right[0, :, :width]
        r_imag = right[1, :, :width]
        dot = functools.partial(jnp.dot, preferred_element_type=F32)
        real = dot(l_real, r_real) + dot(l_imag, r_imag)
        imag = dot(l_real, r_imag) - dot(l_imag, r_real)
        if c == 0:
            acc[0, :, :width] = real
            acc[1, :, :width] = imag
        else:
            acc[0, :, :width] += real
            acc[1, :, :width] += imag

    norm_factor = 1.0 / math.sqrt(6.0 * sites * n)

    def keep(piece, lane):
        for d in range(n):
            for r in range(2):
                part[d, piece, r * owned:(r + 1) * owned, :] = (
                    acc[r, d * owned:(d + 1) * owned, lane:lane + half] * norm_factor
                )

    def hop(g, d, to_slot, to):
        pieces = pl.ds(*groups[g])
        return pltpu.make_async_remote_copy(
            src_ref=slots.at[d, pieces],
            dst_ref=slots.at[to_slot, pieces],
            send_sem=rs_send.at[g, d],
            recv_sem=rs_recv.at[g, to_slot],
            device_id={"space": to},
            device_id_type=MESH,
        )

    def add_and_send(g, d, first, to_slot, to):
        pieces = pl.ds(*groups[g])

        @pl.when(first)
        def _():
            slots[d, pieces] = part[d, pieces].astype(BF16)

        @pl.when(jnp.logical_not(first))
        def _():
            hop(g, d, d, ahead).wait_recv()
            slots[d, pieces] = (slots[d, pieces].astype(F32) + part[d, pieces]).astype(BF16)

        hop(g, d, to_slot, to).start()

    def turns(g, low, high):
        def turn(s, carry):
            @pl.when(me <= s)
            def _():
                far = n - 1 - s + me
                add_and_send(g, far, me == 0, far, ahead)

            @pl.when(n - 1 - me <= s)
            def _():
                near = s - (n - 1 - me)
                add_and_send(g, near, me == n - 1, jnp.where(near == me - 1, n, near), behind)

            return carry

        lax.fori_loop(min(low, n - 1), min(high, n - 1), turn, 0)

    def to_all(d):
        return pltpu.make_async_remote_copy(
            src_ref=outgoing.at[d],
            dst_ref=direct.at[me],
            send_sem=last_send.at[d],
            recv_sem=last_recv.at[me],
            device_id={"space": d},
            device_id_type=MESH,
        )

    def spread(g, t, peer):
        pieces = pl.ds(*groups[g])
        return pltpu.make_async_remote_copy(
            src_ref=gathered.at[t, pieces],
            dst_ref=gathered.at[t, pieces],
            send_sem=ag_send.at[g, peer],
            recv_sem=ag_recv.at[g, t],
            device_id={"tm": peer},
            device_id_type=MESH,
        )

    def give_out(g):
        pieces = pl.ds(*groups[g])
        gathered[my_t, pieces] = part[me, pieces].astype(BF16)
        for peer in peers:
            spread(g, my_t, peer).start()

    def finish(g):
        pieces = pl.ds(*groups[g])

        @pl.when(me > 0)
        def _():
            hop(g, me, me, ahead).wait_recv()
            part[me, pieces] += slots[me, pieces].astype(F32)

        @pl.when(me < n - 1)
        def _():
            hop(g, n, n, ahead).wait_recv()
            part[me, pieces] += slots[n, pieces].astype(F32)

        give_out(g)

    def project_one(g, t):
        low, size = groups[g]
        for piece in range(low, low + size, 2):
            k = piece // 2
            with_real = None
            for p in range(piece, min(piece + 2, low + size)):
                at = (p % 2) * half
                rows = gathered[t, p]
                by_real = jnp.dot(rows, peram[0, 0, at:at + half, :], preferred_element_type=F32)
                by_imag = jnp.dot(rows, peram[0, 1, at:at + half, :], preferred_element_type=F32)
                with_real = by_real if with_real is None else with_real + by_real
                with_imag = by_imag if p == piece else with_imag + by_imag
            real = with_real[:owned] - with_imag[owned:]
            imag = with_imag[:owned] + with_real[owned:]
            if g == 2:
                held[t, 0] = real
                held[t, 1] = imag
                continue
            if g == 3:
                real += held[t, 0]
                imag += held[t, 1]
            lane = k * 2 * modes
            out_p[t, :, lane:lane + modes] = real.astype(BF16)
            out_p[t, :, lane + modes:lane + 2 * modes] = imag.astype(BF16)

    def project(g):
        low, size = groups[g]
        for p in range(low, low + size):
            for r in range(2):
                lane = (p // 2 * 2 + r) * modes + (p % 2) * half
                out_e[:, lane:lane + half] = gathered[my_t, p, r * owned:(r + 1) * owned, :]
        project_one(g, my_t)
        for peer in peers:
            spread(g, peer, peer).wait_recv()
            project_one(g, peer)

    def whole_width(r, b, rows):
        return vec[r, b, rows, :]

    def batch(h, c):
        halos[h][c].wait_recv()
        displace(2, c, lambda r, b, rows: halo[h, r, b, rows, :], half)
        contract(c, half)

    for k in range(2):
        for c in range(batches):
            displace(k, c, whole_width, modes)
            contract(c, modes)
        keep(2 * k, 0)
        keep(2 * k + 1, half)
        turns(k, 0, 1)
        if k == 1:
            turns(0, 1, 2)
        send_batches(1)
    for c in range(batches):
        batch(0, c)
        if c == batches // 2 - 1:
            turns(0, 2, n - 1)
            turns(1, 1, 2)
            send_batches(1)
    keep(4, 0)
    turns(1, 2, n - 1)
    turns(2, 0, 1)
    send_batches(1)
    finish(0)
    load_peram.wait()
    for c in range(batches):
        batch(1, c)
        if c == 0:
            turns(2, 1, 2)
            send_batches(2 * batches)
            finish(1)
        if c == 1:
            turns(2, 2, n - 1)
            project(0)
        if c == batches - 2:
            finish(2)
            project(1)
            project(2)
    keep(5, 0)
    for d in others:
        outgoing[d] = part[d, 5].astype(BF16)
        to_all(d).start()
    for d in others:
        pltpu.make_async_remote_copy(
            src_ref=outgoing.at[d],
            dst_ref=direct.at[d],
            send_sem=last_send.at[d],
            recv_sem=last_recv.at[d],
            device_id={"space": d},
            device_id_type=MESH,
        ).wait_recv()
        part[me, 5] += direct[d].astype(F32)
    give_out(3)
    project(3)

    for copy in halos[0] + halos[1]:
        copy.wait_send()
    for d in others:
        for g in range(3):
            hop(g, d, d, ahead).wait_send()
        to_all(d).wait_send()
    for g in range(4):
        for peer in peers:
            spread(g, my_t, peer).wait_send()


def body(eigvecs, links, momenta, perambulators):
    n = lax.axis_size("space")
    count = lax.axis_size("tm")
    sites, modes = eigvecs.shape[3:]
    owned = modes // n
    half = modes // 2
    batches = sites // BATCH
    vmem = pl.BlockSpec(memory_space=pltpu.VMEM)
    hbm = pl.BlockSpec(memory_space=pltpu.HBM)
    moved_links = jnp.transpose(links, (0, 1, 3, 4, 2, 5))
    elementals, projected = pl.pallas_call(
        functools.partial(kernel, n, count, sites, modes),
        out_shape=(
            jax.ShapeDtypeStruct((owned, 6 * modes), BF16),
            jax.ShapeDtypeStruct((count, owned, 6 * modes), BF16),
        ),
        in_specs=[hbm] * 4,
        out_specs=(vmem, vmem),
        scratch_shapes=[
            pltpu.SMEM(momenta.shape, jnp.int32),
            pltpu.VMEM(moved_links.shape, BF16),
            pltpu.VMEM(perambulators.shape, BF16),
            pltpu.VMEM((2, 3, sites, modes), BF16),
            pltpu.VMEM((2, 2, 3, sites, half), BF16),
            pltpu.VMEM((2, batches, modes, 3 * BATCH), BF16),
            pltpu.VMEM((2, 3 * BATCH, modes), BF16),
            pltpu.VMEM((128, sites), F32),
            pltpu.VMEM((sites, 128), F32),
            pltpu.VMEM((2, modes, modes), F32),
            pltpu.VMEM((n, 6, 2 * owned, half), F32),
            pltpu.VMEM((n + 1, 5, 2 * owned, half), BF16),
            pltpu.VMEM((n, 2 * owned, half), BF16),
            pltpu.VMEM((n, 2 * owned, half), BF16),
            pltpu.VMEM((count, 6, 2 * owned, half), BF16),
            pltpu.VMEM((count, 2, owned, modes), F32),
            pltpu.SemaphoreType.DMA((3,)),
            pltpu.SemaphoreType.DMA,
            pltpu.SemaphoreType.DMA((2, batches)),
            pltpu.SemaphoreType.DMA((2, batches)),
            pltpu.SemaphoreType.DMA((3, n + 1)),
            pltpu.SemaphoreType.DMA((3, n + 1)),
            pltpu.SemaphoreType.DMA((n,)),
            pltpu.SemaphoreType.DMA((n,)),
            pltpu.SemaphoreType.DMA((4, count)),
            pltpu.SemaphoreType.DMA((4, count)),
        ],
        compiler_params=pltpu.CompilerParams(
            collective_id=0, has_side_effects=True, vmem_limit_bytes=62 * 1024 * 1024
        ),
    )(momenta, moved_links, perambulators, eigvecs)
    return (
        elementals.reshape(1, owned, 3, 2, modes),
        projected.reshape(1, count, owned, 3, 2, modes),
    )


def solution(mesh):
    in_specs = (
        P(("ens", "tm"), None, None, "space", None),
        P(("ens", "tm"), None, None, None, None, "space"),
        P(),
        P(("ens", "tm"), None, None, None),
    )
    out_specs = (
        P(("ens", "tm"), "space", None, None, None),
        P(("ens", "tm"), None, "space", None, None, None),
    )
    return jax.shard_map(body, mesh=mesh, in_specs=in_specs, out_specs=out_specs, check_vma=False)
```

```python
import functools
import math

import jax
import jax.numpy as jnp
from jax import lax
from jax.experimental import pallas as pl
from jax.experimental.pallas import tpu as pltpu
from jax.sharding import PartitionSpec as P

LX = 32
LY = 16
BATCH = 128
MESH = pl.DeviceIdType.MESH
F32 = jnp.float32
BF16 = jnp.bfloat16


def kernel(n, count, sites, modes, mom_in, links_in, peram_in, eig, out_e, out_p, mom, links, peram, vec, halo, left_t,
           right, coef, columns, acc, part, slots, outgoing, direct, gathered, held, in_sem, vec_sem, halo_send, halo_recv,
           rs_send, rs_recv, last_send, last_recv, ag_send, ag_recv):
    me = lax.axis_index("space")
    my_t = lax.axis_index("tm")
    owned = modes // n
    half = modes // 2
    batches = sites // BATCH
    behind = lax.rem(me + n - 1, n)
    ahead = lax.rem(me + 1, n)
    others = [lax.rem(me + step, n) for step in range(1, n)]
    peers = [lax.rem(my_t + step, count) for step in range(1, count)]
    groups = ((0, 2), (2, 2), (4, 1), (5, 1))

    barrier = pltpu.get_barrier_semaphore()
    for other in others:
        pl.semaphore_signal(barrier, inc=1, device_id={"space": other}, device_id_type=MESH)
    for peer in peers:
        pl.semaphore_signal(barrier, inc=1, device_id={"tm": peer}, device_id_type=MESH)
    load_mom = pltpu.make_async_copy(mom_in, mom, in_sem.at[0])
    load_links = pltpu.make_async_copy(links_in, links, in_sem.at[1])
    load_peram = pltpu.make_async_copy(peram_in, peram, in_sem.at[2])
    load_vec = pltpu.make_async_copy(eig.at[0], vec, vec_sem)
    for copy in (load_mom, load_links, load_vec, load_peram):
        copy.start()
    pl.semaphore_wait(barrier, n + count - 2)

    halos = [[], []]
    for h in range(2):
        for c in range(batches):
            rows = pl.ds(c * BATCH, BATCH)
            halos[h].append(
                pltpu.make_async_remote_copy(
                    src_ref=eig.at[0, :, :, rows, pl.ds(h * half, half)],
                    dst_ref=halo.at[h, :, :, rows],
                    send_sem=halo_send.at[h, c],
                    recv_sem=halo_recv.at[h, c],
                    device_id={"space": behind},
                    device_id_type=MESH,
                )
            )
    waiting = halos[0] + halos[1]

    def send_batches(number):
        for _ in range(min(number, len(waiting))):
            waiting.pop(0).start()

    send_batches(3)

    site = lax.broadcasted_iota(jnp.int32, (1, sites), 1)
    x_pos = lax.rem(site, LX).astype(F32)
    y_pos = lax.rem(site // LX, LY).astype(F32)
    z_pos = jnp.full((1, sites), me, jnp.int32).astype(F32)
    coef[...] = jnp.zeros_like(coef)
    load_mom.wait()
    load_links.wait()
    for k in range(3):
        weights = [mom[k, axis].astype(F32) for axis in range(3)]
        angle = 2.0 * math.pi * (weights[0] * x_pos / LX + weights[1] * y_pos / LY + weights[2] * z_pos / n)
        cosine = jnp.cos(angle)
        sine = jnp.sin(angle)
        for a in range(3):
            for b in range(3):
                pair = links[0, k, a, b].astype(F32)
                row = ((k * 3 + a) * 3 + b) * 2
                coef[row:row + 1, :] = cosine * pair[0:1] + sine * pair[1:2]
                coef[row + 1:row + 2, :] = cosine * pair[1:2] - sine * pair[0:1]
    for c in range(batches):
        rows = pl.ds(c * BATCH, BATCH)
        columns[rows, :] = jnp.transpose(coef[:, rows])

    load_vec.wait()
    for r in range(2):
        for a in range(3):
            for c in range(batches):
                rows = pl.ds(c * BATCH, BATCH)
                left_t[r, c, :, a * BATCH:(a + 1) * BATCH] = jnp.transpose(vec[r, a, rows, :].astype(F32)).astype(BF16)

    def displace(k, c, read, width):
        def one_row(g, carry):
            strip = c * (BATCH // LX) + g
            source_strip = lax.rem(strip + 1, LY) if k == 1 else strip
            rows = pl.ds(pl.multiple_of(source_strip * LX, LX), LX)
            moved = [[read(r, b, rows).astype(F32) for b in range(3)] for r in range(2)]
            if k == 0:
                moved = [[pltpu.roll(m, LX - 1, 0) for m in pair] for pair in moved]
            factors = columns[pl.ds(pl.multiple_of(strip * LX, LX), LX), :]
            for a in range(3):
                real = None
                imag = None
                for b in range(3):
                    place = ((k * 3 + a) * 3 + b) * 2
                    f_real = factors[:, place:place + 1]
                    f_imag = factors[:, place + 1:place + 2]
                    t_real = f_real * moved[0][b] - f_imag * moved[1][b]
                    t_imag = f_real * moved[1][b] + f_imag * moved[0][b]
                    real = t_real if real is None else real + t_real
                    imag = t_imag if imag is None else imag + t_imag
                to = pl.ds(pl.multiple_of(a * BATCH + g * LX, LX), LX)
                right[0, to, :width] = real.astype(BF16)
                right[1, to, :width] = imag.astype(BF16)
            return carry

        lax.fori_loop(0, BATCH // LX, one_row, 0)

    def contract(c, width):
        l_real = left_t[0, c]
        l_imag = left_t[1, c]
        r_real = right[0, :, :width]
        r_imag = right[1, :, :width]
        dot = functools.partial(jnp.dot, preferred_element_type=F32)
        real = dot(l_real, r_real) + dot(l_imag, r_imag)
        imag = dot(l_real, r_imag) - dot(l_imag, r_real)
        if c == 0:
            acc[0, :, :width] = real
            acc[1, :, :width] = imag
        else:
            acc[0, :, :width] += real
            acc[1, :, :width] += imag

    norm_factor = 1.0 / math.sqrt(6.0 * sites * n)

    def keep(piece, lane):
        for d in range(n):
            for r in range(2):
                part[d, piece, r * owned:(r + 1) * owned, :] = (
                    acc[r, d * owned:(d + 1) * owned, lane:lane + half] * norm_factor
                )

    def hop(g, d, to_slot, to):
        pieces = pl.ds(*groups[g])
        return pltpu.make_async_remote_copy(
            src_ref=slots.at[d, pieces],
            dst_ref=slots.at[to_slot, pieces],
            send_sem=rs_send.at[g, d],
            recv_sem=rs_recv.at[g, to_slot],
            device_id={"space": to},
            device_id_type=MESH,
        )

    def add_and_send(g, d, first, to_slot, to):
        pieces = pl.ds(*groups[g])

        @pl.when(first)
        def _():
            slots[d, pieces] = part[d, pieces].astype(BF16)

        @pl.when(jnp.logical_not(first))
        def _():
            hop(g, d, d, ahead).wait_recv()
            slots[d, pieces] = (slots[d, pieces].astype(F32) + part[d, pieces]).astype(BF16)

        hop(g, d, to_slot, to).start()

    def turns(g, low, high):
        def turn(s, carry):
            @pl.when(me <= s)
            def _():
                far = n - 1 - s + me
                add_and_send(g, far, me == 0, far, ahead)

            @pl.when(n - 1 - me <= s)
            def _():
                near = s - (n - 1 - me)
                add_and_send(g, near, me == n - 1, jnp.where(near == me - 1, n, near), behind)

            return carry

        lax.fori_loop(min(low, n - 1), min(high, n - 1), turn, 0)

    def to_owner(j, source, d):
        return pltpu.make_async_remote_copy(
            src_ref=outgoing.at[j, d],
            dst_ref=direct.at[j, source],
            send_sem=last_send.at[j, d],
            recv_sem=last_recv.at[j, source],
            device_id={"space": d},
            device_id_type=MESH,
        )

    def send_direct(j):
        for d in others:
            outgoing[j, d] = part[d, 4 + j].astype(BF16)
            to_owner(j, me, d).start()

    def finish_direct(j):
        for d in others:
            to_owner(j, d, d).wait_recv()
        total = part[me, 4 + j]
        for d in others:
            total += direct[j, d].astype(F32)
        part[me, 4 + j] = total
        give_out(2 + j)

    def spread(g, t, peer):
        pieces = pl.ds(*groups[g])
        return pltpu.make_async_remote_copy(
            src_ref=gathered.at[t, pieces],
            dst_ref=gathered.at[t, pieces],
            send_sem=ag_send.at[g, peer],
            recv_sem=ag_recv.at[g, t],
            device_id={"tm": peer},
            device_id_type=MESH,
        )

    def give_out(g):
        pieces = pl.ds(*groups[g])
        gathered[my_t, pieces] = part[me, pieces].astype(BF16)
        for peer in peers:
            spread(g, my_t, peer).start()

    def finish(g):
        pieces = pl.ds(*groups[g])

        @pl.when(me > 0)
        def _():
            hop(g, me, me, ahead).wait_recv()
            part[me, pieces] += slots[me, pieces].astype(F32)

        @pl.when(me < n - 1)
        def _():
            hop(g, n, n, ahead).wait_recv()
            part[me, pieces] += slots[n, pieces].astype(F32)

        give_out(g)

    def project_one(g, t):
        low, size = groups[g]
        for piece in range(low, low + size, 2):
            k = piece // 2
            with_real = None
            for p in range(piece, min(piece + 2, low + size)):
                at = (p % 2) * half
                rows = gathered[t, p]
                by_real = jnp.dot(rows, peram[0, 0, at:at + half, :], preferred_element_type=F32)
                by_imag = jnp.dot(rows, peram[0, 1, at:at + half, :], preferred_element_type=F32)
                with_real = by_real if with_real is None else with_real + by_real
                with_imag = by_imag if p == piece else with_imag + by_imag
            real = with_real[:owned] - with_imag[owned:]
            imag = with_imag[:owned] + with_real[owned:]
            if g == 2:
                held[t, 0] = real
                held[t, 1] = imag
                continue
            if g == 3:
                real += held[t, 0]
                imag += held[t, 1]
            lane = k * 2 * modes
            out_p[t, :, lane:lane + modes] = real.astype(BF16)
            out_p[t, :, lane + modes:lane + 2 * modes] = imag.astype(BF16)

    def project(g):
        low, size = groups[g]
        for p in range(low, low + size):
            for r in range(2):
                lane = (p // 2 * 2 + r) * modes + (p % 2) * half
                out_e[:, lane:lane + half] = gathered[my_t, p, r * owned:(r + 1) * owned, :]
        project_one(g, my_t)
        for peer in peers:
            spread(g, peer, peer).wait_recv()
            project_one(g, peer)

    def whole_width(r, b, rows):
        return vec[r, b, rows, :]

    def batch(h, c):
        halos[h][c].wait_recv()
        displace(2, c, lambda r, b, rows: halo[h, r, b, rows, :], half)
        contract(c, half)

    for k in range(2):
        for c in range(batches):
            displace(k, c, whole_width, modes)
            contract(c, modes)
        keep(2 * k, 0)
        keep(2 * k + 1, half)
        turns(k, 0, 1)
        if k == 1:
            turns(0, 1, 2)
        send_batches(1)
    for c in range(batches):
        batch(0, c)
        if c == batches // 2 - 1:
            turns(0, 2, n - 1)
            turns(1, 1, 2)
            send_batches(1)
    keep(4, 0)
    send_direct(0)
    send_batches(1)
    turns(1, 2, n - 1)
    send_batches(2 * batches)
    finish(0)
    load_peram.wait()
    for c in range(batches):
        batch(1, c)
        if c == 0:
            finish(1)
        if c == 1:
            project(0)
            finish_direct(0)
        if c == 2:
            project(1)
    keep(5, 0)
    send_direct(1)
    project(2)
    finish_direct(1)
    project(3)

    for copy in halos[0] + halos[1]:
        copy.wait_send()
    for d in others:
        for g in range(2):
            hop(g, d, d, ahead).wait_send()
            to_owner(g, me, d).wait_send()
    for g in range(4):
        for peer in peers:
            spread(g, my_t, peer).wait_send()


def body(eigvecs, links, momenta, perambulators):
    n = lax.axis_size("space")
    count = lax.axis_size("tm")
    sites, modes = eigvecs.shape[3:]
    owned = modes // n
    half = modes // 2
    batches = sites // BATCH
    vmem = pl.BlockSpec(memory_space=pltpu.VMEM)
    hbm = pl.BlockSpec(memory_space=pltpu.HBM)
    moved_links = jnp.transpose(links, (0, 1, 3, 4, 2, 5))
    elementals, projected = pl.pallas_call(
        functools.partial(kernel, n, count, sites, modes),
        out_shape=(
            jax.ShapeDtypeStruct((owned, 6 * modes), BF16),
            jax.ShapeDtypeStruct((count, owned, 6 * modes), BF16),
        ),
        in_specs=[hbm] * 4,
        out_specs=(vmem, vmem),
        scratch_shapes=[
            pltpu.SMEM(momenta.shape, jnp.int32),
            pltpu.VMEM(moved_links.shape, BF16),
            pltpu.VMEM(perambulators.shape, BF16),
            pltpu.VMEM((2, 3, sites, modes), BF16),
            pltpu.VMEM((2, 2, 3, sites, half), BF16),
            pltpu.VMEM((2, batches, modes, 3 * BATCH), BF16),
            pltpu.VMEM((2, 3 * BATCH, modes), BF16),
            pltpu.VMEM((128, sites), F32),
            pltpu.VMEM((sites, 128), F32),
            pltpu.VMEM((2, modes, modes), F32),
            pltpu.VMEM((n, 6, 2 * owned, half), F32),
            pltpu.VMEM((n + 1, 4, 2 * owned, half), BF16),
            pltpu.VMEM((2, n, 2 * owned, half), BF16),
            pltpu.VMEM((2, n, 2 * owned, half), BF16),
            pltpu.VMEM((count, 6, 2 * owned, half), BF16),
            pltpu.VMEM((count, 2, owned, modes), F32),
            pltpu.SemaphoreType.DMA((3,)),
            pltpu.SemaphoreType.DMA,
            pltpu.SemaphoreType.DMA((2, batches)),
            pltpu.SemaphoreType.DMA((2, batches)),
            pltpu.SemaphoreType.DMA((2, n + 1)),
            pltpu.SemaphoreType.DMA((2, n + 1)),
            pltpu.SemaphoreType.DMA((2, n)),
            pltpu.SemaphoreType.DMA((2, n)),
            pltpu.SemaphoreType.DMA((4, count)),
            pltpu.SemaphoreType.DMA((4, count)),
        ],
        compiler_params=pltpu.CompilerParams(
            collective_id=0, has_side_effects=True, vmem_limit_bytes=62 * 1024 * 1024
        ),
    )(momenta, moved_links, perambulators, eigvecs)
    return (
        elementals.reshape(1, owned, 3, 2, modes),
        projected.reshape(1, count, owned, 3, 2, modes),
    )


def solution(mesh):
    in_specs = (
        P(("ens", "tm"), None, None, "space", None),
        P(("ens", "tm"), None, None, None, None, "space"),
        P(),
        P(("ens", "tm"), None, None, None),
    )
    out_specs = (
        P(("ens", "tm"), "space", None, None, None),
        P(("ens", "tm"), None, "space", None, None, None),
    )
    return jax.shard_map(body, mesh=mesh, in_specs=in_specs, out_specs=out_specs, check_vma=False)
```

```python
import functools
import math

import jax
import jax.numpy as jnp
from jax import lax
from jax.experimental import pallas as pl
from jax.experimental.pallas import tpu as pltpu
from jax.sharding import PartitionSpec as P

LX = 32
LY = 16
BATCH = 128
MESH = pl.DeviceIdType.MESH
F32 = jnp.float32
BF16 = jnp.bfloat16


def kernel(n, count, sites, modes, mom_in, links_in, peram_in, eig, out_e, out_p, mom, links, peram, vec, halo, left_t,
           right, coef, columns, acc, part, slots, outgoing, direct, gathered, held, in_sem, vec_sem, halo_send, halo_recv,
           rs_send, rs_recv, last_send, last_recv, ag_send, ag_recv):
    me = lax.axis_index("space")
    my_t = lax.axis_index("tm")
    owned = modes // n
    half = modes // 2
    batches = sites // BATCH
    behind = lax.rem(me + n - 1, n)
    ahead = lax.rem(me + 1, n)
    others = [lax.rem(me + step, n) for step in range(1, n)]
    peers = [lax.rem(my_t + step, count) for step in range(1, count)]
    groups = ((0, 2), (2, 2), (4, 1), (5, 1))

    barrier = pltpu.get_barrier_semaphore()
    for other in others:
        pl.semaphore_signal(barrier, inc=1, device_id={"space": other}, device_id_type=MESH)
    for peer in peers:
        pl.semaphore_signal(barrier, inc=1, device_id={"tm": peer}, device_id_type=MESH)
    load_mom = pltpu.make_async_copy(mom_in, mom, in_sem.at[0])
    load_links = pltpu.make_async_copy(links_in, links, in_sem.at[1])
    load_peram = pltpu.make_async_copy(peram_in, peram, in_sem.at[2])
    load_vec = pltpu.make_async_copy(eig.at[0], vec, vec_sem)
    for copy in (load_mom, load_links, load_vec, load_peram):
        copy.start()
    pl.semaphore_wait(barrier, n + count - 2)

    halos = [[], []]
    for h in range(2):
        for c in range(batches):
            rows = pl.ds(c * BATCH, BATCH)
            halos[h].append(
                pltpu.make_async_remote_copy(
                    src_ref=eig.at[0, :, :, rows, pl.ds(h * half, half)],
                    dst_ref=halo.at[h, :, :, rows],
                    send_sem=halo_send.at[h, c],
                    recv_sem=halo_recv.at[h, c],
                    device_id={"space": behind},
                    device_id_type=MESH,
                )
            )
    waiting = halos[0] + halos[1]

    def send_batches(number):
        for _ in range(min(number, len(waiting))):
            waiting.pop(0).start()

    send_batches(3)

    site = lax.broadcasted_iota(jnp.int32, (1, sites), 1)
    x_pos = lax.rem(site, LX).astype(F32)
    y_pos = lax.rem(site // LX, LY).astype(F32)
    z_pos = jnp.full((1, sites), me, jnp.int32).astype(F32)
    coef[...] = jnp.zeros_like(coef)
    load_mom.wait()
    load_links.wait()
    for k in range(3):
        weights = [mom[k, axis].astype(F32) for axis in range(3)]
        angle = 2.0 * math.pi * (weights[0] * x_pos / LX + weights[1] * y_pos / LY + weights[2] * z_pos / n)
        cosine = jnp.cos(angle)
        sine = jnp.sin(angle)
        for a in range(3):
            for b in range(3):
                pair = links[0, k, a, b].astype(F32)
                row = ((k * 3 + a) * 3 + b) * 2
                coef[row:row + 1, :] = cosine * pair[0:1] + sine * pair[1:2]
                coef[row + 1:row + 2, :] = cosine * pair[1:2] - sine * pair[0:1]
    for c in range(batches):
        rows = pl.ds(c * BATCH, BATCH)
        columns[rows, :] = jnp.transpose(coef[:, rows])

    load_vec.wait()
    for r in range(2):
        for a in range(3):
            for c in range(batches):
                rows = pl.ds(c * BATCH, BATCH)
                at = (r * 3 + a) * BATCH
                left_t[c, :, at:at + BATCH] = jnp.transpose(vec[r, a, rows, :].astype(F32)).astype(BF16)

    def spread_lanes(column, width):
        narrow = jnp.broadcast_to(column, (LX, 128)).astype(BF16)
        return jnp.concatenate([narrow] * (width // 128), 1)

    def displace(k, c, read, width):
        def one_row(g, carry):
            strip = c * (BATCH // LX) + g
            source_strip = lax.rem(strip + 1, LY) if k == 1 else strip
            rows = pl.ds(pl.multiple_of(source_strip * LX, LX), LX)
            moved = [[read(r, b, rows) for b in range(3)] for r in range(2)]
            if k == 0:
                moved = [[pltpu.roll(m.astype(F32), LX - 1, 0).astype(BF16) for m in pair] for pair in moved]
            factors = columns[pl.ds(pl.multiple_of(strip * LX, LX), LX), :]
            for a in range(3):
                real = None
                imag = None
                for b in range(3):
                    place = ((k * 3 + a) * 3 + b) * 2
                    f_real = spread_lanes(factors[:, place:place + 1], width)
                    f_imag = spread_lanes(factors[:, place + 1:place + 2], width)
                    t_real = f_real * moved[0][b] - f_imag * moved[1][b]
                    t_imag = f_real * moved[1][b] + f_imag * moved[0][b]
                    real = t_real if real is None else real + t_real
                    imag = t_imag if imag is None else imag + t_imag
                to = pl.ds(pl.multiple_of(a * BATCH + g * LX, LX), LX)
                below = pl.ds(pl.multiple_of((3 + a) * BATCH + g * LX, LX), LX)
                right[to, :width] = real
                right[to, width:2 * width] = imag
                right[below, :width] = imag
                right[below, width:2 * width] = -real
            return carry

        lax.fori_loop(0, BATCH // LX, one_row, 0)

    def contract(c, width):
        both = jnp.dot(left_t[c], right[:, :2 * width], preferred_element_type=F32)
        if c == 0:
            acc[:, :2 * width] = both
        else:
            acc[:, :2 * width] += both

    norm_factor = 1.0 / math.sqrt(6.0 * sites * n)

    def keep(piece, lane, width):
        for d in range(n):
            for r in range(2):
                part[d, piece, r * owned:(r + 1) * owned, :] = (
                    acc[d * owned:(d + 1) * owned, r * width + lane:r * width + lane + half] * norm_factor
                )

    def hop(g, d, to_slot, to):
        pieces = pl.ds(*groups[g])
        return pltpu.make_async_remote_copy(
            src_ref=slots.at[d, pieces],
            dst_ref=slots.at[to_slot, pieces],
            send_sem=rs_send.at[g, d],
            recv_sem=rs_recv.at[g, to_slot],
            device_id={"space": to},
            device_id_type=MESH,
        )

    def add_and_send(g, d, first, to_slot, to):
        pieces = pl.ds(*groups[g])

        @pl.when(first)
        def _():
            slots[d, pieces] = part[d, pieces].astype(BF16)

        @pl.when(jnp.logical_not(first))
        def _():
            hop(g, d, d, ahead).wait_recv()
            slots[d, pieces] = (slots[d, pieces].astype(F32) + part[d, pieces]).astype(BF16)

        hop(g, d, to_slot, to).start()

    def turns(g, low, high):
        def turn(s, carry):
            @pl.when(me <= s)
            def _():
                far = n - 1 - s + me
                add_and_send(g, far, me == 0, far, ahead)

            @pl.when(n - 1 - me <= s)
            def _():
                near = s - (n - 1 - me)
                add_and_send(g, near, me == n - 1, jnp.where(near == me - 1, n, near), behind)

            return carry

        lax.fori_loop(min(low, n - 1), min(high, n - 1), turn, 0)

    def to_owner(j, source, d):
        return pltpu.make_async_remote_copy(
            src_ref=outgoing.at[j, d],
            dst_ref=direct.at[j, source],
            send_sem=last_send.at[j, d],
            recv_sem=last_recv.at[j, source],
            device_id={"space": d},
            device_id_type=MESH,
        )

    def send_direct(j):
        for d in others:
            outgoing[j, d] = part[d, 4 + j].astype(BF16)
            to_owner(j, me, d).start()

    def finish_direct(j):
        for d in others:
            to_owner(j, d, d).wait_recv()
        total = part[me, 4 + j]
        for d in others:
            total += direct[j, d].astype(F32)
        part[me, 4 + j] = total
        give_out(2 + j)

    def spread(g, t, peer):
        pieces = pl.ds(*groups[g])
        return pltpu.make_async_remote_copy(
            src_ref=gathered.at[t, pieces],
            dst_ref=gathered.at[t, pieces],
            send_sem=ag_send.at[g, peer],
            recv_sem=ag_recv.at[g, t],
            device_id={"tm": peer},
            device_id_type=MESH,
        )

    def give_out(g):
        pieces = pl.ds(*groups[g])
        gathered[my_t, pieces] = part[me, pieces].astype(BF16)
        for peer in peers:
            spread(g, my_t, peer).start()

    def finish(g):
        pieces = pl.ds(*groups[g])

        @pl.when(me > 0)
        def _():
            hop(g, me, me, ahead).wait_recv()
            part[me, pieces] += slots[me, pieces].astype(F32)

        @pl.when(me < n - 1)
        def _():
            hop(g, n, n, ahead).wait_recv()
            part[me, pieces] += slots[n, pieces].astype(F32)

        give_out(g)

    def project_one(g, t):
        low, size = groups[g]
        for piece in range(low, low + size, 2):
            k = piece // 2
            with_real = None
            for p in range(piece, min(piece + 2, low + size)):
                at = (p % 2) * half
                rows = gathered[t, p]
                by_real = jnp.dot(rows, peram[0, 0, at:at + half, :], preferred_element_type=F32)
                by_imag = jnp.dot(rows, peram[0, 1, at:at + half, :], preferred_element_type=F32)
                with_real = by_real if with_real is None else with_real + by_real
                with_imag = by_imag if p == piece else with_imag + by_imag
            real = with_real[:owned] - with_imag[owned:]
            imag = with_imag[:owned] + with_real[owned:]
            if g == 2:
                held[t, 0] = real
                held[t, 1] = imag
                continue
            if g == 3:
                real += held[t, 0]
                imag += held[t, 1]
            lane = k * 2 * modes
            out_p[t, :, lane:lane + modes] = real.astype(BF16)
            out_p[t, :, lane + modes:lane + 2 * modes] = imag.astype(BF16)

    def project(g):
        low, size = groups[g]
        for p in range(low, low + size):
            for r in range(2):
                lane = (p // 2 * 2 + r) * modes + (p % 2) * half
                out_e[:, lane:lane + half] = gathered[my_t, p, r * owned:(r + 1) * owned, :]
        project_one(g, my_t)
        for peer in peers:
            spread(g, peer, peer).wait_recv()
            project_one(g, peer)

    def whole_width(r, b, rows):
        return vec[r, b, rows, :]

    def batch(h, c):
        halos[h][c].wait_recv()
        displace(2, c, lambda r, b, rows: halo[h, r, b, rows, :], half)
        contract(c, half)

    for k in range(2):
        for c in range(batches):
            displace(k, c, whole_width, modes)
            contract(c, modes)
        keep(2 * k, 0, modes)
        keep(2 * k + 1, half, modes)
        turns(k, 0, 1)
        if k == 1:
            turns(0, 1, 2)
        send_batches(1)
    for c in range(batches):
        batch(0, c)
        if c == batches // 2 - 1:
            turns(0, 2, n - 1)
            turns(1, 1, 2)
            send_batches(1)
    keep(4, 0, half)
    send_direct(0)
    send_batches(1)
    turns(1, 2, n - 1)
    send_batches(2 * batches)
    finish(0)
    load_peram.wait()
    for c in range(batches):
        batch(1, c)
        if c == 0:
            finish(1)
        if c == 1:
            project(0)
            finish_direct(0)
        if c == 2:
            project(1)
    keep(5, 0, half)
    send_direct(1)
    project(2)
    finish_direct(1)
    project(3)

    for copy in halos[0] + halos[1]:
        copy.wait_send()
    for d in others:
        for g in range(2):
            hop(g, d, d, ahead).wait_send()
            to_owner(g, me, d).wait_send()
    for g in range(4):
        for peer in peers:
            spread(g, my_t, peer).wait_send()


def body(eigvecs, links, momenta, perambulators):
    n = lax.axis_size("space")
    count = lax.axis_size("tm")
    sites, modes = eigvecs.shape[3:]
    owned = modes // n
    half = modes // 2
    batches = sites // BATCH
    vmem = pl.BlockSpec(memory_space=pltpu.VMEM)
    hbm = pl.BlockSpec(memory_space=pltpu.HBM)
    moved_links = jnp.transpose(links, (0, 1, 3, 4, 2, 5))
    elementals, projected = pl.pallas_call(
        functools.partial(kernel, n, count, sites, modes),
        out_shape=(
            jax.ShapeDtypeStruct((owned, 6 * modes), BF16),
            jax.ShapeDtypeStruct((count, owned, 6 * modes), BF16),
        ),
        in_specs=[hbm] * 4,
        out_specs=(vmem, vmem),
        scratch_shapes=[
            pltpu.SMEM(momenta.shape, jnp.int32),
            pltpu.VMEM(moved_links.shape, BF16),
            pltpu.VMEM(perambulators.shape, BF16),
            pltpu.VMEM((2, 3, sites, modes), BF16),
            pltpu.VMEM((2, 2, 3, sites, half), BF16),
            pltpu.VMEM((batches, modes, 6 * BATCH), BF16),
            pltpu.VMEM((6 * BATCH, 2 * modes), BF16),
            pltpu.VMEM((128, sites), F32),
            pltpu.VMEM((sites, 128), F32),
            pltpu.VMEM((modes, 2 * modes), F32),
            pltpu.VMEM((n, 6, 2 * owned, half), F32),
            pltpu.VMEM((n + 1, 4, 2 * owned, half), BF16),
            pltpu.VMEM((2, n, 2 * owned, half), BF16),
            pltpu.VMEM((2, n, 2 * owned, half), BF16),
            pltpu.VMEM((count, 6, 2 * owned, half), BF16),
            pltpu.VMEM((count, 2, owned, modes), F32),
            pltpu.SemaphoreType.DMA((3,)),
            pltpu.SemaphoreType.DMA,
            pltpu.SemaphoreType.DMA((2, batches)),
            pltpu.SemaphoreType.DMA((2, batches)),
            pltpu.SemaphoreType.DMA((2, n + 1)),
            pltpu.SemaphoreType.DMA((2, n + 1)),
            pltpu.SemaphoreType.DMA((2, n)),
            pltpu.SemaphoreType.DMA((2, n)),
            pltpu.SemaphoreType.DMA((4, count)),
            pltpu.SemaphoreType.DMA((4, count)),
        ],
        compiler_params=pltpu.CompilerParams(
            collective_id=0, has_side_effects=True, vmem_limit_bytes=62 * 1024 * 1024
        ),
    )(momenta, moved_links, perambulators, eigvecs)
    return (
        elementals.reshape(1, owned, 3, 2, modes),
        projected.reshape(1, count, owned, 3, 2, modes),
    )


def solution(mesh):
    in_specs = (
        P(("ens", "tm"), None, None, "space", None),
        P(("ens", "tm"), None, None, None, None, "space"),
        P(),
        P(("ens", "tm"), None, None, None),
    )
    out_specs = (
        P(("ens", "tm"), "space", None, None, None),
        P(("ens", "tm"), None, "space", None, None, None),
    )
    return jax.shard_map(body, mesh=mesh, in_specs=in_specs, out_specs=out_specs, check_vma=False)
```

```python
import functools
import math

import jax
import jax.numpy as jnp
from jax import lax
from jax.experimental import pallas as pl
from jax.experimental.pallas import tpu as pltpu
from jax.sharding import PartitionSpec as P

LX = 32
LY = 16
BATCH = 128
MESH = pl.DeviceIdType.MESH
F32 = jnp.float32
BF16 = jnp.bfloat16


def kernel(n, count, sites, modes, mom_in, links_in, peram_in, eig, out_e, out_p, mom, links, peram, vec, halo, left_t,
           right, coef, columns, acc, part, slots, outgoing, direct, gathered, held, in_sem, vec_sem, halo_send, halo_recv,
           rs_send, rs_recv, last_send, last_recv, ag_send, ag_recv):
    me = lax.axis_index("space")
    my_t = lax.axis_index("tm")
    owned = modes // n
    half = modes // 2
    batches = sites // BATCH
    behind = lax.rem(me + n - 1, n)
    ahead = lax.rem(me + 1, n)
    others = [lax.rem(me + step, n) for step in range(1, n)]
    peers = [lax.rem(my_t + step, count) for step in range(1, count)]
    groups = ((0, 2), (2, 2), (4, 1), (5, 1))

    barrier = pltpu.get_barrier_semaphore()
    for other in others:
        pl.semaphore_signal(barrier, inc=1, device_id={"space": other}, device_id_type=MESH)
    for peer in peers:
        pl.semaphore_signal(barrier, inc=1, device_id={"tm": peer}, device_id_type=MESH)
    load_mom = pltpu.make_async_copy(mom_in, mom, in_sem.at[0])
    load_links = pltpu.make_async_copy(links_in, links, in_sem.at[1])
    load_peram = pltpu.make_async_copy(peram_in, peram, in_sem.at[2])
    load_vec = pltpu.make_async_copy(eig.at[0], vec, vec_sem)
    for copy in (load_mom, load_links, load_vec, load_peram):
        copy.start()
    pl.semaphore_wait(barrier, n + count - 2)

    halos = [[], []]
    for h in range(2):
        for c in range(batches):
            rows = pl.ds(c * BATCH, BATCH)
            halos[h].append(
                pltpu.make_async_remote_copy(
                    src_ref=eig.at[0, :, :, rows, pl.ds(h * half, half)],
                    dst_ref=halo.at[h, :, :, rows],
                    send_sem=halo_send.at[h, c],
                    recv_sem=halo_recv.at[h, c],
                    device_id={"space": behind},
                    device_id_type=MESH,
                )
            )
    waiting = halos[0] + halos[1]

    def send_batches(number):
        for _ in range(min(number, len(waiting))):
            waiting.pop(0).start()

    send_batches(3)

    site = lax.broadcasted_iota(jnp.int32, (1, sites), 1)
    x_pos = lax.rem(site, LX).astype(F32)
    y_pos = lax.rem(site // LX, LY).astype(F32)
    z_pos = jnp.full((1, sites), me, jnp.int32).astype(F32)
    coef[...] = jnp.zeros_like(coef)
    load_mom.wait()
    load_links.wait()
    for k in range(3):
        weights = [mom[k, axis].astype(F32) for axis in range(3)]
        angle = 2.0 * math.pi * (weights[0] * x_pos / LX + weights[1] * y_pos / LY + weights[2] * z_pos / n)
        cosine = jnp.cos(angle)
        sine = jnp.sin(angle)
        for a in range(3):
            for b in range(3):
                pair = links[0, k, a, b].astype(F32)
                row = ((k * 3 + a) * 3 + b) * 2
                coef[row:row + 1, :] = cosine * pair[0:1] + sine * pair[1:2]
                coef[row + 1:row + 2, :] = cosine * pair[1:2] - sine * pair[0:1]
    for c in range(batches):
        rows = pl.ds(c * BATCH, BATCH)
        columns[rows, :] = jnp.transpose(coef[:, rows])

    load_vec.wait()
    for r in range(2):
        for a in range(3):
            for c in range(batches):
                rows = pl.ds(c * BATCH, BATCH)
                at = (r * 3 + a) * BATCH
                left_t[c, :, at:at + BATCH] = jnp.transpose(vec[r, a, rows, :].astype(F32)).astype(BF16)

    def spread_lanes(column, width):
        narrow = jnp.broadcast_to(column, (LX, 128)).astype(BF16)
        return jnp.concatenate([narrow] * (width // 128), 1)

    def displace(k, c, read, width):
        def one_row(g, carry):
            strip = c * (BATCH // LX) + g
            source_strip = lax.rem(strip + 1, LY) if k == 1 else strip
            rows = pl.ds(pl.multiple_of(source_strip * LX, LX), LX)
            moved = [[read(r, b, rows) for b in range(3)] for r in range(2)]
            if k == 0:
                moved = [[pltpu.roll(m.astype(F32), LX - 1, 0).astype(BF16) for m in pair] for pair in moved]
            factors = columns[pl.ds(pl.multiple_of(strip * LX, LX), LX), :]
            for a in range(3):
                real = None
                imag = None
                for b in range(3):
                    place = ((k * 3 + a) * 3 + b) * 2
                    f_real = spread_lanes(factors[:, place:place + 1], width)
                    f_imag = spread_lanes(factors[:, place + 1:place + 2], width)
                    t_real = f_real * moved[0][b] - f_imag * moved[1][b]
                    t_imag = f_real * moved[1][b] + f_imag * moved[0][b]
                    real = t_real if real is None else real + t_real
                    imag = t_imag if imag is None else imag + t_imag
                to = pl.ds(pl.multiple_of(a * BATCH + g * LX, LX), LX)
                below = pl.ds(pl.multiple_of((3 + a) * BATCH + g * LX, LX), LX)
                right[to, :width] = real
                right[to, width:2 * width] = imag
                right[below, :width] = imag
                right[below, width:2 * width] = -real
            return carry

        lax.fori_loop(0, BATCH // LX, one_row, 0)

    def contract(c, width):
        both = jnp.dot(left_t[c], right[:, :2 * width], preferred_element_type=F32)
        if c == 0:
            acc[:, :2 * width] = both
        else:
            acc[:, :2 * width] += both

    norm_factor = 1.0 / math.sqrt(6.0 * sites * n)

    def keep(piece, lane, width):
        for d in range(n):
            for r in range(2):
                part[d, piece, r * owned:(r + 1) * owned, :] = (
                    acc[d * owned:(d + 1) * owned, r * width + lane:r * width + lane + half] * norm_factor
                )

    def hop(g, d, to_slot, to):
        pieces = pl.ds(*groups[g])
        return pltpu.make_async_remote_copy(
            src_ref=slots.at[d, pieces],
            dst_ref=slots.at[to_slot, pieces],
            send_sem=rs_send.at[g, d],
            recv_sem=rs_recv.at[g, to_slot],
            device_id={"space": to},
            device_id_type=MESH,
        )

    def add_and_send(g, d, first, to_slot, to):
        pieces = pl.ds(*groups[g])

        @pl.when(first)
        def _():
            slots[d, pieces] = part[d, pieces].astype(BF16)

        @pl.when(jnp.logical_not(first))
        def _():
            hop(g, d, d, ahead).wait_recv()
            slots[d, pieces] = (slots[d, pieces].astype(F32) + part[d, pieces]).astype(BF16)

        hop(g, d, to_slot, to).start()

    def turns(g, low, high):
        def turn(s, carry):
            @pl.when(me <= s)
            def _():
                far = n - 1 - s + me
                add_and_send(g, far, me == 0, far, ahead)

            @pl.when(n - 1 - me <= s)
            def _():
                near = s - (n - 1 - me)
                add_and_send(g, near, me == n - 1, jnp.where(near == me - 1, n, near), behind)

            return carry

        lax.fori_loop(min(low, n - 1), min(high, n - 1), turn, 0)

    def to_owner(j, source, d):
        return pltpu.make_async_remote_copy(
            src_ref=outgoing.at[j, d],
            dst_ref=direct.at[j, source],
            send_sem=last_send.at[j, d],
            recv_sem=last_recv.at[j, source],
            device_id={"space": d},
            device_id_type=MESH,
        )

    def send_direct(j):
        for d in others:
            outgoing[j, d] = part[d, 4 + j].astype(BF16)
            to_owner(j, me, d).start()

    def finish_direct(j):
        for d in others:
            to_owner(j, d, d).wait_recv()
        total = part[me, 4 + j]
        for d in others:
            total += direct[j, d].astype(F32)
        part[me, 4 + j] = total
        give_out(2 + j)

    def spread(g, t, peer):
        pieces = pl.ds(*groups[g])
        return pltpu.make_async_remote_copy(
            src_ref=gathered.at[t, pieces],
            dst_ref=gathered.at[t, pieces],
            send_sem=ag_send.at[g, peer],
            recv_sem=ag_recv.at[g, t],
            device_id={"tm": peer},
            device_id_type=MESH,
        )

    def give_out(g):
        pieces = pl.ds(*groups[g])
        gathered[my_t, pieces] = part[me, pieces].astype(BF16)
        for peer in peers:
            spread(g, my_t, peer).start()

    def finish(g):
        pieces = pl.ds(*groups[g])

        @pl.when(me > 0)
        def _():
            hop(g, me, me, ahead).wait_recv()
            part[me, pieces] += slots[me, pieces].astype(F32)

        @pl.when(me < n - 1)
        def _():
            hop(g, n, n, ahead).wait_recv()
            part[me, pieces] += slots[n, pieces].astype(F32)

        give_out(g)

    def project_one(g, t):
        low, size = groups[g]
        for piece in range(low, low + size, 2):
            k = piece // 2
            with_real = None
            for p in range(piece, min(piece + 2, low + size)):
                at = (p % 2) * half
                rows = gathered[t, p]
                by_real = jnp.dot(rows, peram[0, 0, at:at + half, :], preferred_element_type=F32)
                by_imag = jnp.dot(rows, peram[0, 1, at:at + half, :], preferred_element_type=F32)
                with_real = by_real if with_real is None else with_real + by_real
                with_imag = by_imag if p == piece else with_imag + by_imag
            real = with_real[:owned] - with_imag[owned:]
            imag = with_imag[:owned] + with_real[owned:]
            if g == 2:
                held[t, 0] = real
                held[t, 1] = imag
                continue
            if g == 3:
                real += held[t, 0]
                imag += held[t, 1]
            out_p[0, t, :, k] = jnp.stack([real, imag], 1).astype(BF16)

    def project(g):
        low, size = groups[g]
        for p in range(low, low + size):
            lane = (p % 2) * half
            both = [gathered[my_t, p, r * owned:(r + 1) * owned, :].astype(F32) for r in range(2)]
            out_e[0, :, p // 2, :, lane:lane + half] = jnp.stack(both, 1).astype(BF16)
        project_one(g, my_t)
        for peer in peers:
            spread(g, peer, peer).wait_recv()
            project_one(g, peer)

    def whole_width(r, b, rows):
        return vec[r, b, rows, :]

    def batch(h, c):
        halos[h][c].wait_recv()
        displace(2, c, lambda r, b, rows: halo[h, r, b, rows, :], half)
        contract(c, half)

    for k in range(2):
        for c in range(batches):
            displace(k, c, whole_width, modes)
            contract(c, modes)
        keep(2 * k, 0, modes)
        keep(2 * k + 1, half, modes)
        turns(k, 0, 1)
        if k == 1:
            turns(0, 1, 2)
        send_batches(1)
    for c in range(batches):
        batch(0, c)
        if c == batches // 2 - 1:
            turns(0, 2, n - 1)
            turns(1, 1, 2)
            send_batches(1)
    keep(4, 0, half)
    send_direct(0)
    send_batches(1)
    turns(1, 2, n - 1)
    send_batches(2 * batches)
    finish(0)
    load_peram.wait()
    for c in range(batches):
        batch(1, c)
        if c == 0:
            finish(1)
        if c == 1:
            project(0)
            finish_direct(0)
        if c == 2:
            project(1)
    keep(5, 0, half)
    send_direct(1)
    project(2)
    finish_direct(1)
    project(3)

    for copy in halos[0] + halos[1]:
        copy.wait_send()
    for d in others:
        for g in range(2):
            hop(g, d, d, ahead).wait_send()
            to_owner(g, me, d).wait_send()
    for g in range(4):
        for peer in peers:
            spread(g, my_t, peer).wait_send()


def body(eigvecs, links, momenta, perambulators):
    n = lax.axis_size("space")
    count = lax.axis_size("tm")
    sites, modes = eigvecs.shape[3:]
    owned = modes // n
    half = modes // 2
    batches = sites // BATCH
    vmem = pl.BlockSpec(memory_space=pltpu.VMEM)
    hbm = pl.BlockSpec(memory_space=pltpu.HBM)
    moved_links = jnp.transpose(links, (0, 1, 3, 4, 2, 5))
    elementals, projected = pl.pallas_call(
        functools.partial(kernel, n, count, sites, modes),
        out_shape=(
            jax.ShapeDtypeStruct((1, owned, 3, 2, modes), BF16),
            jax.ShapeDtypeStruct((1, count, owned, 3, 2, modes), BF16),
        ),
        in_specs=[hbm] * 4,
        out_specs=(vmem, vmem),
        scratch_shapes=[
            pltpu.SMEM(momenta.shape, jnp.int32),
            pltpu.VMEM(moved_links.shape, BF16),
            pltpu.VMEM(perambulators.shape, BF16),
            pltpu.VMEM((2, 3, sites, modes), BF16),
            pltpu.VMEM((2, 2, 3, sites, half), BF16),
            pltpu.VMEM((batches, modes, 6 * BATCH), BF16),
            pltpu.VMEM((6 * BATCH, 2 * modes), BF16),
            pltpu.VMEM((128, sites), F32),
            pltpu.VMEM((sites, 128), F32),
            pltpu.VMEM((modes, 2 * modes), F32),
            pltpu.VMEM((n, 6, 2 * owned, half), F32),
            pltpu.VMEM((n + 1, 4, 2 * owned, half), BF16),
            pltpu.VMEM((2, n, 2 * owned, half), BF16),
            pltpu.VMEM((2, n, 2 * owned, half), BF16),
            pltpu.VMEM((count, 6, 2 * owned, half), BF16),
            pltpu.VMEM((count, 2, owned, modes), F32),
            pltpu.SemaphoreType.DMA((3,)),
            pltpu.SemaphoreType.DMA,
            pltpu.SemaphoreType.DMA((2, batches)),
            pltpu.SemaphoreType.DMA((2, batches)),
            pltpu.SemaphoreType.DMA((2, n + 1)),
            pltpu.SemaphoreType.DMA((2, n + 1)),
            pltpu.SemaphoreType.DMA((2, n)),
            pltpu.SemaphoreType.DMA((2, n)),
            pltpu.SemaphoreType.DMA((4, count)),
            pltpu.SemaphoreType.DMA((4, count)),
        ],
        compiler_params=pltpu.CompilerParams(
            collective_id=0, has_side_effects=True, vmem_limit_bytes=62 * 1024 * 1024
        ),
    )(momenta, moved_links, perambulators, eigvecs)
    return elementals, projected


def solution(mesh):
    in_specs = (
        P(("ens", "tm"), None, None, "space", None),
        P(("ens", "tm"), None, None, None, None, "space"),
        P(),
        P(("ens", "tm"), None, None, None),
    )
    out_specs = (
        P(("ens", "tm"), "space", None, None, None),
        P(("ens", "tm"), None, "space", None, None, None),
    )
    return jax.shard_map(body, mesh=mesh, in_specs=in_specs, out_specs=out_specs, check_vma=False)
```

```python
import functools
import math

import jax
import jax.numpy as jnp
from jax import lax
from jax.experimental import pallas as pl
from jax.experimental.pallas import tpu as pltpu
from jax.sharding import PartitionSpec as P

LX = 32
LY = 16
BATCH = 128
MESH = pl.DeviceIdType.MESH
F32 = jnp.float32
BF16 = jnp.bfloat16


def kernel(n, count, sites, modes, mom_in, links_in, peram_in, eig, out_e, out_p, mom, links, peram, vec, halo, left_t,
           right, coef, columns, acc, part, slots, outgoing, direct, gathered, held, in_sem, vec_sem, halo_send, halo_recv,
           rs_send, rs_recv, last_send, last_recv, ag_send, ag_recv):
    me = lax.axis_index("space")
    my_t = lax.axis_index("tm")
    owned = modes // n
    half = modes // 2
    batches = sites // BATCH
    behind = lax.rem(me + n - 1, n)
    ahead = lax.rem(me + 1, n)
    others = [lax.rem(me + step, n) for step in range(1, n)]
    peers = [lax.rem(my_t + step, count) for step in range(1, count)]
    groups = ((0, 2), (2, 2), (4, 1), (5, 1))

    barrier = pltpu.get_barrier_semaphore()
    for other in others:
        pl.semaphore_signal(barrier, inc=1, device_id={"space": other}, device_id_type=MESH)
    for peer in peers:
        pl.semaphore_signal(barrier, inc=1, device_id={"tm": peer}, device_id_type=MESH)
    load_mom = pltpu.make_async_copy(mom_in, mom, in_sem.at[0])
    load_links = pltpu.make_async_copy(links_in, links, in_sem.at[1])
    load_peram = pltpu.make_async_copy(peram_in, peram, in_sem.at[2])
    load_vec = pltpu.make_async_copy(eig.at[0], vec, vec_sem)
    for copy in (load_mom, load_links, load_vec, load_peram):
        copy.start()
    pl.semaphore_wait(barrier, n + count - 2)

    halos = [[], []]
    for h in range(2):
        for c in range(batches):
            rows = pl.ds(c * BATCH, BATCH)
            halos[h].append(
                pltpu.make_async_remote_copy(
                    src_ref=eig.at[0, :, :, rows, pl.ds(h * half, half)],
                    dst_ref=halo.at[h, :, :, rows],
                    send_sem=halo_send.at[h, c],
                    recv_sem=halo_recv.at[h, c],
                    device_id={"space": behind},
                    device_id_type=MESH,
                )
            )
    waiting = halos[0] + halos[1]

    def send_batches(number):
        for _ in range(min(number, len(waiting))):
            waiting.pop(0).start()

    send_batches(3)

    site = lax.broadcasted_iota(jnp.int32, (1, sites), 1)
    x_pos = lax.rem(site, LX).astype(F32)
    y_pos = lax.rem(site // LX, LY).astype(F32)
    z_pos = jnp.full((1, sites), me, jnp.int32).astype(F32)
    coef[...] = jnp.zeros_like(coef)
    load_mom.wait()
    load_links.wait()
    for k in range(3):
        weights = [mom[k, axis].astype(F32) for axis in range(3)]
        angle = 2.0 * math.pi * (weights[0] * x_pos / LX + weights[1] * y_pos / LY + weights[2] * z_pos / n)
        cosine = jnp.cos(angle)
        sine = jnp.sin(angle)
        for a in range(3):
            for b in range(3):
                pair = links[0, k, a, b].astype(F32)
                row = ((k * 3 + a) * 3 + b) * 2
                coef[row:row + 1, :] = cosine * pair[0:1] + sine * pair[1:2]
                coef[row + 1:row + 2, :] = cosine * pair[1:2] - sine * pair[0:1]
    for c in range(batches):
        rows = pl.ds(c * BATCH, BATCH)
        columns[rows, :] = jnp.transpose(coef[:, rows])

    load_vec.wait()
    for r in range(2):
        for a in range(3):
            for c in range(batches):
                rows = pl.ds(c * BATCH, BATCH)
                at = (r * 3 + a) * BATCH
                left_t[c, :, at:at + BATCH] = jnp.transpose(vec[r, a, rows, :].astype(F32)).astype(BF16)

    def spread_lanes(column, width):
        narrow = jnp.broadcast_to(column, (LX, 128)).astype(BF16)
        return jnp.concatenate([narrow] * (width // 128), 1)

    def displace(k, c, read, width):
        def one_row(g, carry):
            strip = c * (BATCH // LX) + g
            source_strip = lax.rem(strip + 1, LY) if k == 1 else strip
            rows = pl.ds(pl.multiple_of(source_strip * LX, LX), LX)
            moved = [[read(r, b, rows) for b in range(3)] for r in range(2)]
            if k == 0:
                moved = [[pltpu.roll(m.astype(F32), LX - 1, 0).astype(BF16) for m in pair] for pair in moved]
            factors = columns[pl.ds(pl.multiple_of(strip * LX, LX), LX), :]
            for a in range(3):
                real = None
                imag = None
                for b in range(3):
                    place = ((k * 3 + a) * 3 + b) * 2
                    f_real = spread_lanes(factors[:, place:place + 1], width)
                    f_imag = spread_lanes(factors[:, place + 1:place + 2], width)
                    t_real = f_real * moved[0][b] - f_imag * moved[1][b]
                    t_imag = f_real * moved[1][b] + f_imag * moved[0][b]
                    real = t_real if real is None else real + t_real
                    imag = t_imag if imag is None else imag + t_imag
                to = pl.ds(pl.multiple_of(a * BATCH + g * LX, LX), LX)
                below = pl.ds(pl.multiple_of((3 + a) * BATCH + g * LX, LX), LX)
                right[to, :width] = real
                right[to, width:2 * width] = imag
                right[below, :width] = imag
                right[below, width:2 * width] = -real
            return carry

        lax.fori_loop(0, BATCH // LX, one_row, 0)

    def contract(c, width):
        both = jnp.dot(left_t[c], right[:, :2 * width], preferred_element_type=F32)
        if c == 0:
            acc[:, :2 * width] = both
        else:
            acc[:, :2 * width] += both

    norm_factor = 1.0 / math.sqrt(6.0 * sites * n)

    def keep(piece, lane, width):
        for d in range(n):
            for r in range(2):
                part[d, piece, r * owned:(r + 1) * owned, :] = (
                    acc[d * owned:(d + 1) * owned, r * width + lane:r * width + lane + half] * norm_factor
                )

    def hop(g, d, to_slot, to):
        pieces = pl.ds(*groups[g])
        return pltpu.make_async_remote_copy(
            src_ref=slots.at[d, pieces],
            dst_ref=slots.at[to_slot, pieces],
            send_sem=rs_send.at[g, d],
            recv_sem=rs_recv.at[g, to_slot],
            device_id={"space": to},
            device_id_type=MESH,
        )

    def add_and_send(g, d, first, to_slot, to):
        pieces = pl.ds(*groups[g])

        @pl.when(first)
        def _():
            slots[d, pieces] = part[d, pieces].astype(BF16)

        @pl.when(jnp.logical_not(first))
        def _():
            hop(g, d, d, ahead).wait_recv()
            slots[d, pieces] = (slots[d, pieces].astype(F32) + part[d, pieces]).astype(BF16)

        hop(g, d, to_slot, to).start()

    def turns(g, low, high):
        def turn(s, carry):
            @pl.when(me <= s)
            def _():
                far = n - 1 - s + me
                add_and_send(g, far, me == 0, far, ahead)

            @pl.when(n - 1 - me <= s)
            def _():
                near = s - (n - 1 - me)
                add_and_send(g, near, me == n - 1, jnp.where(near == me - 1, n, near), behind)

            return carry

        lax.fori_loop(min(low, n - 1), min(high, n - 1), turn, 0)

    def to_owner(j, source, d):
        return pltpu.make_async_remote_copy(
            src_ref=outgoing.at[j, d],
            dst_ref=direct.at[j, source],
            send_sem=last_send.at[j, d],
            recv_sem=last_recv.at[j, source],
            device_id={"space": d},
            device_id_type=MESH,
        )

    def send_direct(j):
        for d in others:
            outgoing[j, d] = part[d, 4 + j].astype(BF16)
            to_owner(j, me, d).start()

    def finish_direct(j):
        for d in others:
            to_owner(j, d, d).wait_recv()
        total = part[me, 4 + j]
        for d in others:
            total += direct[j, d].astype(F32)
        part[me, 4 + j] = total
        give_out(2 + j)

    def spread(g, t, peer):
        pieces = pl.ds(*groups[g])
        return pltpu.make_async_remote_copy(
            src_ref=gathered.at[t, pieces],
            dst_ref=gathered.at[t, pieces],
            send_sem=ag_send.at[g, peer],
            recv_sem=ag_recv.at[g, t],
            device_id={"tm": peer},
            device_id_type=MESH,
        )

    def give_out(g):
        pieces = pl.ds(*groups[g])
        gathered[my_t, pieces] = part[me, pieces].astype(BF16)
        for peer in peers:
            spread(g, my_t, peer).start()

    def finish(g):
        pieces = pl.ds(*groups[g])

        @pl.when(me > 0)
        def _():
            hop(g, me, me, ahead).wait_recv()
            part[me, pieces] += slots[me, pieces].astype(F32)

        @pl.when(me < n - 1)
        def _():
            hop(g, n, n, ahead).wait_recv()
            part[me, pieces] += slots[n, pieces].astype(F32)

        give_out(g)

    def project_one(g, t):
        low, size = groups[g]
        for piece in range(low, low + size, 2):
            k = piece // 2
            with_real = None
            for p in range(piece, min(piece + 2, low + size)):
                at = (p % 2) * half
                rows = gathered[t, p]
                by_real = jnp.dot(rows, peram[0, 0, at:at + half, :], preferred_element_type=F32)
                by_imag = jnp.dot(rows, peram[0, 1, at:at + half, :], preferred_element_type=F32)
                with_real = by_real if with_real is None else with_real + by_real
                with_imag = by_imag if p == piece else with_imag + by_imag
            real = with_real[:owned] - with_imag[owned:]
            imag = with_imag[:owned] + with_real[owned:]
            if g == 2:
                held[t, 0] = real
                held[t, 1] = imag
                continue
            if g == 3:
                real += held[t, 0]
                imag += held[t, 1]
            lane = k * 2 * modes
            out_p[t, :, lane:lane + modes] = real.astype(BF16)
            out_p[t, :, lane + modes:lane + 2 * modes] = imag.astype(BF16)

    def project(g):
        low, size = groups[g]
        for p in range(low, low + size):
            for r in range(2):
                lane = (p // 2 * 2 + r) * modes + (p % 2) * half
                out_e[:, lane:lane + half] = gathered[my_t, p, r * owned:(r + 1) * owned, :]
        project_one(g, my_t)
        for peer in peers:
            spread(g, peer, peer).wait_recv()
            project_one(g, peer)

    def whole_width(r, b, rows):
        return vec[r, b, rows, :]

    def batch(h, c):
        halos[h][c].wait_recv()
        displace(2, c, lambda r, b, rows: halo[h, r, b, rows, :], half)
        contract(c, half)

    for k in range(2):
        for c in range(batches):
            displace(k, c, whole_width, modes)
            contract(c, modes)
        keep(2 * k, 0, modes)
        keep(2 * k + 1, half, modes)
        turns(k, 0, 1)
        if k == 1:
            turns(0, 1, 2)
        send_batches(1)
    for c in range(batches):
        batch(0, c)
        if c == batches // 2 - 1:
            turns(0, 2, n - 1)
            turns(1, 1, 2)
            send_batches(1)
    keep(4, 0, half)
    send_batches(1)
    turns(1, 2, n - 1)
    send_batches(2 * batches)
    send_direct(0)
    finish(0)
    load_peram.wait()
    for c in range(batches):
        batch(1, c)
        if c == 0:
            finish(1)
        if c == 1:
            project(0)
        if c == 2:
            project(1)
    keep(5, 0, half)
    send_direct(1)
    finish_direct(0)
    finish_direct(1)
    project(2)
    project(3)

    for copy in halos[0] + halos[1]:
        copy.wait_send()
    for d in others:
        for g in range(2):
            hop(g, d, d, ahead).wait_send()
            to_owner(g, me, d).wait_send()
    for g in range(4):
        for peer in peers:
            spread(g, my_t, peer).wait_send()


def body(eigvecs, links, momenta, perambulators):
    n = lax.axis_size("space")
    count = lax.axis_size("tm")
    sites, modes = eigvecs.shape[3:]
    owned = modes // n
    half = modes // 2
    batches = sites // BATCH
    vmem = pl.BlockSpec(memory_space=pltpu.VMEM)
    hbm = pl.BlockSpec(memory_space=pltpu.HBM)
    moved_links = jnp.transpose(links, (0, 1, 3, 4, 2, 5))
    elementals, projected = pl.pallas_call(
        functools.partial(kernel, n, count, sites, modes),
        out_shape=(
            jax.ShapeDtypeStruct((owned, 6 * modes), BF16),
            jax.ShapeDtypeStruct((count, owned, 6 * modes), BF16),
        ),
        in_specs=[hbm] * 4,
        out_specs=(vmem, vmem),
        scratch_shapes=[
            pltpu.SMEM(momenta.shape, jnp.int32),
            pltpu.VMEM(moved_links.shape, BF16),
            pltpu.VMEM(perambulators.shape, BF16),
            pltpu.VMEM((2, 3, sites, modes), BF16),
            pltpu.VMEM((2, 2, 3, sites, half), BF16),
            pltpu.VMEM((batches, modes, 6 * BATCH), BF16),
            pltpu.VMEM((6 * BATCH, 2 * modes), BF16),
            pltpu.VMEM((128, sites), F32),
            pltpu.VMEM((sites, 128), F32),
            pltpu.VMEM((modes, 2 * modes), F32),
            pltpu.VMEM((n, 6, 2 * owned, half), F32),
            pltpu.VMEM((n + 1, 4, 2 * owned, half), BF16),
            pltpu.VMEM((2, n, 2 * owned, half), BF16),
            pltpu.VMEM((2, n, 2 * owned, half), BF16),
            pltpu.VMEM((count, 6, 2 * owned, half), BF16),
            pltpu.VMEM((count, 2, owned, modes), F32),
            pltpu.SemaphoreType.DMA((3,)),
            pltpu.SemaphoreType.DMA,
            pltpu.SemaphoreType.DMA((2, batches)),
            pltpu.SemaphoreType.DMA((2, batches)),
            pltpu.SemaphoreType.DMA((2, n + 1)),
            pltpu.SemaphoreType.DMA((2, n + 1)),
            pltpu.SemaphoreType.DMA((2, n)),
            pltpu.SemaphoreType.DMA((2, n)),
            pltpu.SemaphoreType.DMA((4, count)),
            pltpu.SemaphoreType.DMA((4, count)),
        ],
        compiler_params=pltpu.CompilerParams(
            collective_id=0, has_side_effects=True, vmem_limit_bytes=62 * 1024 * 1024
        ),
    )(momenta, moved_links, perambulators, eigvecs)
    return (
        elementals.reshape(1, owned, 3, 2, modes),
        projected.reshape(1, count, owned, 3, 2, modes),
    )


def solution(mesh):
    in_specs = (
        P(("ens", "tm"), None, None, "space", None),
        P(("ens", "tm"), None, None, None, None, "space"),
        P(),
        P(("ens", "tm"), None, None, None),
    )
    out_specs = (
        P(("ens", "tm"), "space", None, None, None),
        P(("ens", "tm"), None, "space", None, None, None),
    )
    return jax.shard_map(body, mesh=mesh, in_specs=in_specs, out_specs=out_specs, check_vma=False)
```
